32 devices in a mesh: group: 2 (over x), tile: 16 (over z, y, core).
Axes of the slice: x: 2, y: 2, z: 4, core: 2. Of those that a mesh axis runs over, the one named last changes fastest.
Arguments:
- background: float32 [8, 32, 256, 128], P('group', 'tile'), parts along dimension 0, may hold values from -6 to 6
- near_body: float32 [8, 64, 128, 128], P('group', 'tile'), parts along dimension 0, may hold values from -6 to 6
- bg_kappa: float32 [64, 256, 128], P(('group', 'tile')), parts along dimension 0, may hold values from 0.2 to 2
- nb_kappa: float32 [128, 128, 128], P(('group', 'tile')), parts along dimension 0, may hold values from 0.2 to 2
- nb_recv_cell: int32 [32768], P(('group', 'tile')), parts along dimension 0, may hold values from 0 to 65535, as said below
- nb_donor_owner: int32 [32768, 1], P(('group', 'tile')), parts along dimension 0, may hold values from 0 to 15; in each aligned block of 1024 rows (0 to 1023, 1024 to 2047, ...) at most 128 rows name the same one
- nb_donor_base: int32 [32768], P(('group', 'tile')), parts along dimension 0, may hold values from 0 to 32638, as said below
- nb_donor_frac: float32 [3, 32768], P(None, ('group', 'tile')), parts along dimension 1, may hold values from 0 to 1
- bg_recv_cell: int32 [32768], P(('group', 'tile')), parts along dimension 0, may hold values from 0 to 65535, as said below
- bg_donor_owner: int32 [32768, 1], P(('group', 'tile')), parts along dimension 0, may hold values from 0 to 15; in each aligned block of 1024 rows (0 to 1023, 1024 to 2047, ...) at most 128 rows name the same one
- bg_donor_base: int32 [32768], P(('group', 'tile')), parts along dimension 0, may hold values from 0 to 49022, as said below
- bg_donor_frac: float32 [3, 32768], P(None, ('group', 'tile')), parts along dimension 1, may hold values from 0 to 1
Outputs:
- new_background: float32 [8, 32, 256, 128], P('group', 'tile'), parts along dimension 0
- new_near_body: float32 [8, 64, 128, 128], P('group', 'tile'), parts along dimension 0
The draws below stay inside these ranges and needn't reach their ends.
There are 2 independent parts, one for each index of `group`. The reference program is written for one: setup_inputs(seed, part) draws one part's arguments, and reference() takes and returns one part's arrays. A program takes and returns all parts, laid end to end along the dimension named above; each array names one. Nothing has to cross between parts.
Inputs may be any that keep to these rules, and one draw needn't show every extreme that they name: `nb_recv_cell`: receptor cells are distinct within each device's 1024 rows. `bg_recv_cell`: receptor cells are distinct within each device's 1024 rows. `nb_donor_owner`: in the rows of one device no owner is named more than 128 times. `bg_donor_owner`: in the rows of one device no owner is named more than 128 times. `nb_donor_base`: the corner's indices are at most 0, 254 and 126. `bg_donor_base`: the corner's indices are at most 2, 126 and 126.
All inputs are finite; a program needn't handle non-finite values.
Results may differ from the reference program's by a relative error of at most 0.0003.
Values sent between devices are 32-bit elements; how exact they have to be, the bound alone decides.
No kernel may reach another device: no remote copies, remote signals or barrier semaphores. Data moves between devices by JAX's collectives and lax.ppermute only.
A program may use at most 192 MiB of HBM per device.

```python
import math
import jax
import jax.numpy as jnp
import numpy as np

C = 4
BX = 2
BY = 256
BZ = 128
NI = 4
NJ = 128
NK = 128
REC = 1024
CAP = 128
N_TILE = 16


def receptor_cells(key, total_cells):
    subkeys = jax.random.split(key, N_TILE)

    def device_cells(subkey):
        shuffled = jax.random.permutation(subkey, total_cells - 2)[:REC - 2] + 1
        return jnp.concatenate([jnp.array([0, total_cells - 1], jnp.int32), shuffled.astype(jnp.int32)])
    return jax.vmap(device_cells)(subkeys).reshape(-1)


def corner_bases(key, span_x, span_y, span_z):
    first, second, third = jax.random.split(key, 3)
    index_x = jax.random.randint(first, (N_TILE * REC,), 0, span_x - 1)
    index_y = jax.random.randint(second, (N_TILE * REC,), 0, span_y - 1)
    index_z = jax.random.randint(third, (N_TILE * REC,), 0, span_z - 1)
    flattened = ((index_x * span_y + index_y) * span_z + index_z).astype(jnp.int32)
    highest = (span_x - 2) * span_y * span_z + (span_y - 2) * span_z + span_z - 2
    return flattened.at[0].set(highest).at[1].set(0)


def draw_nb_recv_cell(key, part):
    key = jax.random.fold_in(key, 11)
    return receptor_cells(key, NI * NJ * NK)


def draw_bg_recv_cell(key, part):
    key = jax.random.fold_in(key, 12)
    return receptor_cells(key, BX * BY * BZ)


def draw_nb_donor_base(key, part):
    key = jax.random.fold_in(key, 13)
    return corner_bases(key, BX, BY, BZ)


def draw_bg_donor_base(key, part):
    key = jax.random.fold_in(key, 14)
    return corner_bases(key, NI, NJ, NK)


def block_levels(stream_key, shape, cuts, least, largest):
    loudness = 1.0
    for position, shards_of in cuts:
        heights = jax.random.uniform(jax.random.fold_in(jax.random.fold_in(stream_key, 6), position), (shards_of,), jnp.float32, least / len(cuts), largest / len(cuts))
        loudness = loudness * jnp.repeat(jnp.exp(heights), shape[position] // shards_of).reshape((-1,) + (1,) * (len(shape) - 1 - position))
    return loudness


def deal_out(own_key, own, number, rows, number_of, top, limit, slope):
    order = jax.random.permutation(own_key, number_of)
    crowded, usual = portions_of(number_of, rows * top, limit, slope, True), portions_of(number_of, rows * top, limit, slope, False)
    places = jnp.arange(number_of)

    def named(tallies, turn):
        used = int((tallies > 0).sum())
        fixed = max(1, used // 4)
        moved = fixed + (places - fixed + turn * (used - fixed)) % max(1, number_of - fixed)
        return jnp.zeros((number_of,), jnp.int32).at[order[jnp.where(places < fixed, places, moved)]].set(jnp.asarray(tallies, jnp.int32))

    tallies = jnp.where(number % 4 == 0, named(crowded, number // 4), named(usual, number - number // 4 - 1))
    mixed = jax.random.permutation(jax.random.fold_in(own, 3), number_of)
    source_of, receiver = mixed[0:number_of // 2 * 2:2], mixed[1:number_of // 2 * 2:2]
    margin = jnp.minimum(tallies[source_of] - 1, limit - tallies[receiver]) // 2
    margin = jnp.where((source_of == order[0]) | (receiver == order[0]) | (tallies[receiver] == 0), 0, jnp.maximum(margin, 0))
    moved = jax.random.randint(jax.random.fold_in(own, 4), (number_of // 2,), 0, 1 << 20) % (margin + 1)
    tallies = tallies.at[source_of].add(-moved).at[receiver].add(moved)
    labels = jnp.searchsorted(jnp.cumsum(tallies), jnp.arange(rows * top), side="right").astype(jnp.int32)
    table = labels.reshape(top, rows).T
    table = table[jax.random.permutation(jax.random.fold_in(own, 1), rows)]
    turn = jax.random.randint(jax.random.fold_in(own, 2), (rows, 1), 0, top)
    return jnp.take_along_axis(table, (jnp.arange(top)[None, :] + turn) % top, axis=1)


def portions_of(number_of, total, most, lean, full):
    loads = [(1 << 20) // math.isqrt(grade ** lean) + 1 for grade in range(1, number_of + 1)]
    largest = most if full else min(most, max(-(-total // number_of), total * loads[0] // sum(loads)))
    least = 1 if total - largest >= number_of - 1 else 0
    given, spare = [largest] + [least] * (number_of - 1), total - largest - least * (number_of - 1)
    while spare > 0:
        candidates = [i for i in range(1, number_of) if given[i] < largest] or [i for i in range(1, number_of) if given[i] < most]
        mass, budget = sum([loads[i] for i in candidates]), spare
        for i in candidates:
            extra = min(most - given[i], max(1, budget * loads[i] // mass), spare)
            given[i] = given[i] + extra
            spare = spare - extra
    return np.array(given)


def scatter_about(stream_key, shape, spread, most, cuts=(), kind=jnp.bfloat16):
    gain = block_levels(stream_key, shape, cuts, -0.22, 0.18) if cuts else 1.0
    values = jax.random.normal(stream_key, shape, jnp.float32) * spread * gain
    return jnp.minimum(jnp.maximum(values, -most), most).astype(kind)


def setup_inputs(seed: int = 0, part: int = 0) -> dict:
    key_list = jax.random.split(jax.random.key(seed), 13)
    own_keys = jax.random.split(jax.random.fold_in(key_list[12], part), 13)
    background = scatter_about(own_keys[0], (C, BX * N_TILE, BY, BZ), 1.0, 6.0, ((1, 16),), jnp.float32)
    near_body = scatter_about(own_keys[1], (C, NI * N_TILE, NJ, NK), 1.0, 6.0, ((1, 16),), jnp.float32)
    bg_kappa = jnp.clip(jnp.exp(math.log(2.0) - 2.3025851 * jax.random.uniform(own_keys[2], (BX * N_TILE, BY, BZ), jnp.float32) ** block_levels(own_keys[2], (BX * N_TILE, BY, BZ), ((0, 16),), -0.2, 0.2)), 0.2, 2.0)
    nb_kappa = jnp.clip(jnp.exp(math.log(2.0) - 2.3025851 * jax.random.uniform(own_keys[3], (NI * N_TILE, NJ, NK), jnp.float32) ** block_levels(own_keys[3], (NI * N_TILE, NJ, NK), ((0, 16),), -0.2, 0.2)), 0.2, 2.0)
    nb_recv_cell = draw_nb_recv_cell(jax.random.fold_in(jax.random.fold_in(key_list[12], part), 71), part)
    nb_donor_owner_keys = jax.random.split(jax.random.fold_in(own_keys[5], 1), (REC * N_TILE) // REC)
    nb_donor_owner_turns = jax.random.permutation(jax.random.fold_in(own_keys[5], 3), (REC * N_TILE) // REC)
    nb_donor_owner = jax.vmap(lambda own, number: deal_out(jax.random.fold_in(own_keys[5], 2), own, number, REC, N_TILE, 1, CAP, 2))(nb_donor_owner_keys, nb_donor_owner_turns).reshape((REC * N_TILE, 1))
    nb_donor_base = draw_nb_donor_base(jax.random.fold_in(jax.random.fold_in(key_list[12], part), 71), part)
    nb_donor_frac = jnp.clip(1.0 * jax.random.uniform(own_keys[7], (3, REC * N_TILE), jnp.float32) ** block_levels(own_keys[7], (3, REC * N_TILE), ((1, 16),), -0.2, 0.2), 0.0, 1.0)
    bg_recv_cell = draw_bg_recv_cell(jax.random.fold_in(jax.random.fold_in(key_list[12], part), 71), part)
    bg_donor_owner_keys = jax.random.split(jax.random.fold_in(own_keys[9], 1), (REC * N_TILE) // REC)
    bg_donor_owner_turns = jax.random.permutation(jax.random.fold_in(own_keys[9], 3), (REC * N_TILE) // REC)
    bg_donor_owner = jax.vmap(lambda own, number: deal_out(jax.random.fold_in(own_keys[9], 2), own, number, REC, N_TILE, 1, CAP, 2))(bg_donor_owner_keys, bg_donor_owner_turns).reshape((REC * N_TILE, 1))
    bg_donor_base = draw_bg_donor_base(jax.random.fold_in(jax.random.fold_in(key_list[12], part), 71), part)
    bg_donor_frac = jnp.clip(1.0 * jax.random.uniform(own_keys[11], (3, REC * N_TILE), jnp.float32) ** block_levels(own_keys[11], (3, REC * N_TILE), ((1, 16),), -0.2, 0.2), 0.0, 1.0)
    return dict(background=background, near_body=near_body, bg_kappa=bg_kappa, nb_kappa=nb_kappa, nb_recv_cell=nb_recv_cell, nb_donor_owner=nb_donor_owner, nb_donor_base=nb_donor_base, nb_donor_frac=nb_donor_frac, bg_recv_cell=bg_recv_cell, bg_donor_owner=bg_donor_owner, bg_donor_base=bg_donor_base, bg_donor_frac=bg_donor_frac)


time_step = 0.05


def trilinear(fraction):
    result = []
    for corner in range(8):
        along_x = corner // 4
        along_y = (corner // 2) % 2
        along_z = corner % 2
        factor_x = fraction[0] if along_x else 1.0 - fraction[0]
        factor_y = fraction[1] if along_y else 1.0 - fraction[1]
        factor_z = fraction[2] if along_z else 1.0 - fraction[2]
        result.append(factor_x * factor_y * factor_z)
    return result


def corner_offset(corner, span_y, span_z):
    return (corner // 4) * span_y * span_z + ((corner // 2) % 2) * span_z + corner % 2


def interpolate(flattened, donor_index, fraction, span_y, span_z):
    weights = trilinear(fraction)
    summed = weights[0] * flattened[:, donor_index + corner_offset(0, span_y, span_z)]
    for corner in range(1, 8):
        summed = summed + weights[corner] * flattened[:, donor_index + corner_offset(corner, span_y, span_z)]
    return summed


def advance(fields, diffusivity, behind, ahead):
    rightward = jnp.roll(fields, -1, axis=-2)
    leftward = jnp.roll(fields, 1, axis=-2)
    widths = [(0, 0)] * (fields.ndim - 1) + [(1, 1)]
    padded = jnp.pad(fields, widths)
    upward = padded[..., 2:]
    downward = padded[..., :-2]
    laplace = behind + ahead + rightward + leftward + upward + downward - 6.0 * fields
    transport = fields[0:1] * (ahead - behind) + fields[1:2] * (rightward - leftward) + fields[2:3] * (upward - downward)
    return fields + time_step * (diffusivity[None] * laplace - 0.5 * transport)


def reference(background, near_body, bg_kappa, nb_kappa, nb_recv_cell, nb_donor_owner, nb_donor_base, nb_donor_frac, bg_recv_cell, bg_donor_owner, bg_donor_base, bg_donor_frac):
    tile_cells = BX * BY * BZ
    block_cells = NI * NJ * NK
    tile_flat = background.reshape(C, -1)
    block_flat = near_body.reshape(C, -1)
    device_of_row = (jnp.arange(N_TILE * REC, dtype=jnp.int32) // REC).astype(jnp.int32)
    nb_values = interpolate(tile_flat, nb_donor_owner[:, 0] * tile_cells + nb_donor_base, nb_donor_frac, BY, BZ)
    bg_values = interpolate(block_flat, bg_donor_owner[:, 0] * block_cells + bg_donor_base, bg_donor_frac, NJ, NK)
    block_set = block_flat.at[:, device_of_row * block_cells + nb_recv_cell].set(nb_values)
    tile_set = tile_flat.at[:, device_of_row * tile_cells + bg_recv_cell].set(bg_values)
    tile_set = tile_set.reshape(background.shape)
    tile_pad = jnp.pad(tile_set, ((0, 0), (1, 1), (0, 0), (0, 0)))
    new_background = advance(tile_set, bg_kappa, tile_pad[:, :-2], tile_pad[:, 2:])
    block_set = block_set.reshape(C, N_TILE, NI, NJ, NK)
    block_pad = jnp.pad(block_set, ((0, 0), (0, 0), (1, 1), (0, 0), (0, 0)))
    block_diffusivity = nb_kappa.reshape(N_TILE, NI, NJ, NK)
    new_blocks = advance(block_set, block_diffusivity, block_pad[:, :, :-2], block_pad[:, :, 2:])
    return new_background, new_blocks.reshape(near_body.shape)
```

```python
import functools

import jax
import jax.numpy as jnp
from jax import lax
from jax.experimental import pallas as pl
from jax.experimental.pallas import tpu as pltpu
from jax.sharding import PartitionSpec as P

time_step = 0.05
LANES = 128
F32 = jnp.float32
BF16 = jnp.bfloat16
NT = (((1,), (1,)), ((), ()))
NN = (((1,), (0,)), ((), ()))


def iota(shape, dim):
    return lax.broadcasted_iota(jnp.int32, shape, dim)


def split(value, pieces):
    result = []
    for _ in range(pieces):
        piece = value.astype(BF16)
        result.append(piece)
        value = value - piece.astype(F32)
    return result


def pack_kernel(
    peers, capacity, nb_owner, nb_base, nb_frac, bg_owner, bg_base, bg_frac,
    request, slots, left, right,
):
    blocks = nb_owner.shape[0]
    groups = request.shape[0]
    before = iota((LANES, 2 * LANES), 0) < iota((LANES, 2 * LANES), 1)
    triangle = jnp.where(before, 1.0, 0.0).astype(BF16)
    for grid, (owner, base, frac) in enumerate(
        ((nb_owner, nb_base, nb_frac), (bg_owner, bg_base, bg_frac))
    ):
        owners = owner[...]
        hits = [
            jnp.where(iota((peers, LANES), 0) == owners[b : b + 1], 1.0, 0.0)
            for b in range(blocks)
        ]
        counts = lax.dot_general(
            jnp.concatenate(hits, axis=0).astype(BF16), triangle, NN, preferred_element_type=F32
        )
        carry = jnp.zeros((peers, LANES), F32)
        bases = base[...]
        high = (bases >> 8).astype(F32)
        low = (bases & 255).astype(F32)
        fractions = frac[...]
        pieces = []
        rest = fractions
        for _ in range(3):
            piece = rest.astype(BF16).astype(F32)
            pieces.append(piece)
            rest = rest - piece
        for b in range(blocks):
            rows = slice(b * peers, (b + 1) * peers)
            lanes = slice(b * LANES, (b + 1) * LANES)
            running = counts[rows, :LANES] + carry
            carry = carry + counts[rows, LANES:]
            rank = jnp.sum(hits[b] * running, axis=0, keepdims=True).astype(jnp.int32)
            slot = owners[b : b + 1] * capacity + rank
            slots[grid * blocks + b : grid * blocks + b + 1, :] = slot.astype(F32)
            group = slot >> 7
            place = slot & (LANES - 1)
            right[:, lanes] = jnp.where(iota((LANES, LANES), 0) == place, 1.0, 0.0).astype(BF16)
            chosen = iota((groups, LANES), 0) == group
            fields = [high[b : b + 1], low[b : b + 1]]
            fields += [piece[d : d + 1, lanes] for d in range(3) for piece in pieces]
            for index, field in enumerate(fields):
                left[index * groups : (index + 1) * groups, lanes] = jnp.where(
                    chosen, field, 0.0
                ).astype(BF16)
        packed = lax.dot_general(left[...], right[...], NT, preferred_element_type=F32)
        part = [packed[i * groups : (i + 1) * groups] for i in range(11)]
        request[:, 4 * grid, :] = part[0] * 256.0 + part[1]
        for d in range(3):
            request[:, 4 * grid + 1 + d, :] = part[2 + 3 * d] + part[3 + 3 * d] + part[4 + 3 * d]


def table_kernel(tile, block, tile_table, block_table):
    for source, table in ((tile, tile_table), (block, block_table)):
        components, rows, depth = source.shape
        for c in range(components):
            for start in range(0, rows, LANES):
                turned = source[c, start : start + LANES, :].T
                coarse, fine = split(turned, 2)
                table[c * depth : (c + 1) * depth, start : start + LANES] = coarse
                table[c * depth : (c + 1) * depth, rows + start : rows + start + LANES] = fine


def donor_kernel(spans, width, request, tile_table, block_table, values, weights):
    senders = request.shape[0]
    step = width // LANES

    def chunk(n, _):
        first = n * step
        for grid, table in enumerate((tile_table, block_table)):
            span_x, span_y, span_z = spans[grid]
            rows = span_x * span_y
            fields = [
                jnp.concatenate(
                    [request[first + s, 4 * grid + f, :][None] for s in range(step)], axis=1
                )
                for f in range(4)
            ]
            base = fields[0].astype(jnp.int32)
            place_z = base % span_z
            row = base // span_z
            place_y = row % span_y
            place_x = row // span_y
            frac_x, frac_y, frac_z = fields[1:]
            lower = iota((span_y, width), 0) == place_y
            upper = iota((span_y, width), 0) == place_y + 1
            for x in range(span_x):
                factor = jnp.where(
                    place_x == x, 1.0 - frac_x, jnp.where(place_x == x - 1, frac_x, 0.0)
                )
                weight = jnp.where(
                    lower, factor * (1.0 - frac_y), jnp.where(upper, factor * frac_y, 0.0)
                )
                coarse, fine = split(weight, 2)
                weights[x * span_y : (x + 1) * span_y, :] = coarse
                weights[rows + x * span_y : rows + (x + 1) * span_y, :] = fine
            coarse_table = table[:, :rows]
            mixed = (
                lax.dot_general(coarse_table, weights[:rows, :], NN, preferred_element_type=F32)
                + lax.dot_general(coarse_table, weights[rows:, :], NN, preferred_element_type=F32)
                + lax.dot_general(
                    table[:, rows:], weights[:rows, :], NN, preferred_element_type=F32
                )
            )
            along = iota((span_z, width), 0)
            weight_z = jnp.where(
                along == place_z, 1.0 - frac_z, jnp.where(along == place_z + 1, frac_z, 0.0)
            )
            for c in range(4):
                total = jnp.sum(
                    mixed[c * span_z : (c + 1) * span_z] * weight_z, axis=0, keepdims=True
                )
                for s in range(step):
                    values[first + s, 4 * grid + c, :] = total[0, s * LANES : (s + 1) * LANES]
        return 0

    lax.fori_loop(0, senders // step, chunk, 0)


def receive(k, slots, cells, span_y, planes, returned, places, rows_hit, spots):
    groups = returned.shape[0]
    blocks = slots.shape[0]
    lhs = []
    for c in range(4):
        lhs += split(returned[:, 4 * k + c, :], 3)
    lhs = jnp.concatenate([lhs[3 * c + s] for s in range(3) for c in range(4)], axis=0)
    depth = LANES
    values = []
    for b in range(blocks):
        lanes = slice(b * LANES, (b + 1) * LANES)
        slot = slots[b : b + 1].astype(jnp.int32)
        cell = cells[b : b + 1].astype(jnp.int32)
        group = slot >> 7
        place = slot & (LANES - 1)
        onehot = jnp.where(iota((LANES, LANES), 0) == place, 1.0, 0.0).astype(BF16)
        found = lax.dot_general(lhs, onehot, NN, preferred_element_type=F32)
        size = 4 * groups
        found = found[:size] + found[size : 2 * size] + found[2 * size :]
        chosen = iota((groups, LANES), 0) == group
        z = cell % depth
        row = cell // depth
        y = row % span_y
        x = row // span_y
        mark = iota((depth, LANES), 0) == z
        spots[0, :, lanes] = jnp.where(mark, 1.0, 0.0).astype(BF16)
        for c in range(4):
            value = jnp.sum(
                jnp.where(chosen, found[c * groups : (c + 1) * groups], 0.0),
                axis=0,
                keepdims=True,
            )
            coarse = value.astype(BF16).astype(F32)
            fine = value - coarse
            spots[1 + c, :, lanes] = jnp.where(mark, coarse, 0.0).astype(BF16)
            spots[5 + c, :, lanes] = jnp.where(mark, fine, 0.0).astype(BF16)
        for index, plane in enumerate(planes):
            hit = jnp.where(x == plane, y, -1)
            rows_hit[index * span_y : (index + 1) * span_y, lanes] = jnp.where(
                iota((span_y, LANES), 0) == hit, 1.0, 0.0
            ).astype(BF16)


def place_values(count, rows_hit, spots, old, fields, first):
    span_y = old.shape[2]
    for index in range(count):
        hit = rows_hit[index * span_y : (index + 1) * span_y, :]
        mask = lax.dot_general(hit, spots[0], NT, preferred_element_type=F32) > 0.5
        for c in range(0, 4, 2):
            pair = spots[1 + c : 3 + c].reshape(2 * LANES, -1)
            rest = spots[5 + c : 7 + c].reshape(2 * LANES, -1)
            placed = lax.dot_general(
                hit, pair, NT, preferred_element_type=F32
            ) + lax.dot_general(hit, rest, NT, preferred_element_type=F32)
            for d in range(2):
                merged = jnp.where(
                    mask, placed[:, d * LANES : (d + 1) * LANES], old[c + d, index]
                )
                fields[c + d, first + index, 8 : 8 + span_y, :] = merged
                fields[c + d, first + index, 0:8, :] = merged[span_y - 8 :]
                fields[c + d, first + index, 8 + span_y :, :] = merged[:8]


def advance(fields, kappa, result, size):
    planes, span_y, depth = kappa.shape
    lane = iota((size, depth), 1)
    for x in range(planes):
        for start in range(0, span_y, size):
            scale = time_step * kappa[x, start : start + size, :]
            speeds = [
                (-0.5 * time_step) * fields[d, x + 1, 8 + start : 8 + start + size, :]
                for d in range(3)
            ]
            for c in range(4):
                here = fields[c, x + 1, 8 + start : 8 + start + size, :]
                left = fields[c, x + 1, 7 + start : 7 + start + size, :]
                right = fields[c, x + 1, 9 + start : 9 + start + size, :]
                behind = fields[c, x, 8 + start : 8 + start + size, :]
                ahead = fields[c, x + 2, 8 + start : 8 + start + size, :]
                up = jnp.where(lane == depth - 1, 0.0, pltpu.roll(here, depth - 1, 1))
                down = jnp.where(lane == 0, 0.0, pltpu.roll(here, 1, 1))
                laplace = (behind + ahead) + (left + right) + (up + down) - 6.0 * here
                result[c, x, start : start + size, :] = (
                    here
                    + scale * laplace
                    + speeds[0] * (ahead - behind)
                    + speeds[1] * (right - left)
                    + speeds[2] * (up - down)
                )


def finish_kernel(
    returned, slots, nb_cells, bg_cells, low_halo, high_halo, background, near_body,
    bg_kappa, nb_kappa, new_background, new_near_body,
    tile_fields, block_fields, rows_hit, spots,
):
    blocks = nb_cells.shape[0]
    span_x, span_y = background.shape[1:3]
    block_x, block_y = near_body.shape[1:3]
    components = background.shape[0]
    layer = components * span_y
    receive(
        0, slots[:blocks, :], nb_cells[...], block_y, range(block_x), returned, None, rows_hit, spots
    )
    place_values(block_x, rows_hit, spots, near_body, block_fields, 1)
    for c in range(components):
        block_fields[c, 0] = jnp.zeros(block_fields.shape[2:], F32)
        block_fields[c, block_x + 1] = jnp.zeros(block_fields.shape[2:], F32)
    advance(block_fields, nb_kappa, new_near_body, 32)
    receive(
        1, slots[blocks:, :], bg_cells[...], span_y, range(span_x), returned, None, rows_hit, spots
    )
    place_values(span_x, rows_hit, spots, background, tile_fields, 1)
    for k, halo, plane, target in (
        (2, low_halo, span_x - 1, 0), (3, high_halo, 0, span_x + 1),
    ):
        receive(
            k, halo[layer : layer + blocks, :], halo[layer + blocks :, :], span_y, [plane],
            returned, None, rows_hit, spots,
        )
        old = halo[:layer, :].reshape(components, 1, span_y, LANES)
        place_values(1, rows_hit, spots, old, tile_fields, target)
    advance(tile_fields, bg_kappa, new_background, 32)


def call(kernel, outs, scratch, flops, *operands):
    moved = sum(a.size * a.dtype.itemsize for a in operands)
    moved += sum(o.size * o.dtype.itemsize for o in outs)
    return pl.pallas_call(
        kernel,
        out_shape=outs,
        scratch_shapes=scratch,
        compiler_params=pltpu.CompilerParams(vmem_limit_bytes=40 * 1024 * 1024),
        cost_estimate=pl.CostEstimate(flops=flops, bytes_accessed=moved, transcendentals=0),
    )(*operands)


def body(
    background, near_body, bg_kappa, nb_kappa,
    nb_recv_cell, nb_donor_owner, nb_donor_base, nb_donor_frac,
    bg_recv_cell, bg_donor_owner, bg_donor_base, bg_donor_frac,
):
    peers = lax.axis_size("tile")
    components, span_x, span_y, depth = background.shape
    block_x, block_y = near_body.shape[1:3]
    receptors = nb_recv_cell.shape[0]
    capacity = 2 * receptors // peers
    blocks = receptors // LANES
    groups = peers * capacity // LANES
    shape = jax.ShapeDtypeStruct

    def to_peers(array):
        if capacity == LANES:
            return array
        rows = array.shape[1]
        array = array.reshape(groups, rows, LANES // capacity, capacity)
        return array.transpose(0, 2, 1, 3).reshape(peers, rows, capacity)

    def to_groups(array):
        if capacity == LANES:
            return array
        rows = array.shape[1]
        array = array.reshape(groups, LANES // capacity, rows, capacity)
        return array.transpose(0, 2, 1, 3).reshape(groups, rows, LANES)

    def lines(array):
        return array.reshape(blocks, LANES)

    request, slots = call(
        functools.partial(pack_kernel, peers, capacity),
        [shape((groups, 8, LANES), F32), shape((2 * blocks, LANES), F32)],
        [pltpu.VMEM((11 * groups, receptors), BF16), pltpu.VMEM((LANES, receptors), BF16)],
        100_000_000,
        lines(nb_donor_owner), lines(nb_donor_base), nb_donor_frac,
        lines(bg_donor_owner), lines(bg_donor_base), bg_donor_frac,
    )
    request = to_groups(lax.all_to_all(to_peers(request), "tile", 0, 0, tiled=True))

    description = jnp.concatenate([slots[blocks:], lines(bg_recv_cell).astype(F32)], axis=0)
    forward = [(i, i + 1) for i in range(peers - 1)]
    backward = [(target, source) for source, target in forward]

    def edge(plane):
        return jnp.concatenate(
            [background[:, plane].reshape(components * span_y, depth), description], axis=0
        )

    low_halo = lax.ppermute(edge(span_x - 1), "tile", forward)
    high_halo = lax.ppermute(edge(0), "tile", backward)

    rows = span_x * span_y
    block_rows = block_x * block_y
    tile_table, block_table = call(
        table_kernel,
        [
            shape((components * depth, 2 * rows), BF16),
            shape((components * depth, 2 * block_rows), BF16),
        ],
        [],
        1_000_000,
        background.reshape(components, rows, depth),
        near_body.reshape(components, block_rows, depth),
    )
    width = 2 * LANES
    spans = ((span_x, span_y, depth), (block_x, block_y, depth))
    (values,) = call(
        functools.partial(donor_kernel, spans, width),
        [shape((groups, 8, LANES), F32)],
        [pltpu.VMEM((2 * max(rows, block_rows), width), BF16)],
        2_000_000_000,
        request, tile_table, block_table,
    )
    values = to_peers(values)
    empty = jnp.zeros((1, 4) + values.shape[2:], F32)
    from_low = jnp.concatenate([empty, values[:-1, 4:]], axis=0)
    from_high = jnp.concatenate([values[1:, 4:], empty], axis=0)
    response = jnp.concatenate([values, from_low, from_high], axis=1)
    returned = to_groups(lax.all_to_all(response, "tile", 0, 0, tiled=True))
    return tuple(
        call(
            finish_kernel,
            [shape(background.shape, F32), shape(near_body.shape, F32)],
            [
                pltpu.VMEM((components, span_x + 2, span_y + 16, depth), F32),
                pltpu.VMEM((components, block_x + 2, block_y + 16, depth), F32),
                pltpu.VMEM((max(rows, block_rows), receptors), BF16),
                pltpu.VMEM((9, depth, receptors), BF16),
            ],
            2_000_000_000,
            returned, slots, lines(nb_recv_cell), lines(bg_recv_cell), low_halo, high_halo,
            background, near_body, bg_kappa, nb_kappa,
        )
    )


def solution(mesh):
    both = ("group", "tile")
    field = P("group", "tile", None, None)
    row = (P(both), P(both, None), P(both), P(None, both))
    return jax.shard_map(
        body,
        mesh=mesh,
        in_specs=(field, field, P(both, None, None), P(both, None, None)) + row + row,
        out_specs=(field, field),
        check_vma=False,
    )
```

```python
import functools

import jax
import jax.numpy as jnp
from jax import lax
from jax.experimental import pallas as pl
from jax.experimental.pallas import tpu as pltpu
from jax.sharding import PartitionSpec as P

time_step = 0.05
LANES = 128
F32 = jnp.float32
BF16 = jnp.bfloat16
F8 = jnp.float8_e4m3fn
FINE = 512.0
SCALE = 64.0
NT = (((1,), (1,)), ((), ()))
NN = (((1,), (0,)), ((), ()))
MIB = 1024 * 1024


def iota(shape, dim):
    return lax.broadcasted_iota(jnp.int32, shape, dim)


def small_iota(shape, dim):
    return iota(shape, dim).astype(F32).astype(BF16)


def small(value):
    return value.astype(F32).astype(BF16)


def split(value, pieces):
    result = []
    for _ in range(pieces):
        piece = value.astype(BF16)
        result.append(piece)
        value = value - piece.astype(F32)
    return result


def parity():
    return lax.rem(lax.axis_index("tile"), 2)


def pack_kernel(
    peers, capacity, nb_owner, nb_base, nb_frac, nb_cell, bg_owner, bg_base, bg_frac, bg_cell,
    background, request, slots, inner_edge, outer_edge,
    integers, fractions, left, right, sems,
):
    blocks = integers.shape[1]
    groups = request.shape[0]
    components, span_x, span_y, _ = background.shape
    layer = components * span_y
    odd = parity()
    edges = []
    for k, (edge, plane) in enumerate(
        ((inner_edge, (1 - odd) * (span_x - 1)), (outer_edge, odd * (span_x - 1)))
    ):
        for c in range(components):
            edges.append(
                pltpu.make_async_copy(
                    background.at[c, plane], edge.at[pl.ds(c * span_y, span_y)],
                    sems.at[7 + k * components + c],
                )
            )
    loads = [
        pltpu.make_async_copy(source, integers.at[i], sems.at[i])
        for i, source in enumerate((nb_owner, nb_base, bg_owner, bg_base, bg_cell))
    ]
    loads += [
        pltpu.make_async_copy(source, fractions.at[i], sems.at[5 + i])
        for i, source in enumerate((nb_frac, bg_frac))
    ]
    for copy in loads + edges:
        copy.start()
    before = iota((LANES, 2 * LANES), 0) < iota((LANES, 2 * LANES), 1)
    triangle = jnp.where(before, 1.0, 0.0).astype(BF16)
    for copy in loads:
        copy.wait()
    for grid in range(2):
        owners = integers[2 * grid]
        hits = [
            jnp.where(iota((peers, LANES), 0) == owners[b : b + 1], 1.0, 0.0)
            for b in range(blocks)
        ]
        counts = lax.dot_general(
            jnp.concatenate(hits, axis=0).astype(BF16), triangle, NN, preferred_element_type=F32
        )
        carry = jnp.zeros((peers, LANES), F32)
        bases = integers[2 * grid + 1]
        high = (bases >> 8).astype(F32)
        low = (bases & 255).astype(F32)
        pieces = []
        rest = fractions[grid]
        for _ in range(3):
            piece = rest.astype(BF16).astype(F32)
            pieces.append(piece)
            rest = rest - piece
        for b in range(blocks):
            rows = slice(b * peers, (b + 1) * peers)
            lanes = slice(b * LANES, (b + 1) * LANES)
            running = counts[rows, :LANES] + carry
            carry = carry + counts[rows, LANES:]
            rank = jnp.sum(hits[b] * running, axis=0, keepdims=True).astype(jnp.int32)
            slot = owners[b : b + 1] * capacity + rank
            slots[grid * blocks + b : grid * blocks + b + 1, :] = slot.astype(F32)
            if grid:
                for edge in (inner_edge, outer_edge):
                    edge[layer + b : layer + b + 1, :] = slot.astype(F32)
            group = slot >> 7
            place = slot & (LANES - 1)
            right[grid, :, lanes] = jnp.where(
                iota((LANES, LANES), 0) == place, 1.0, 0.0
            ).astype(BF16)
            chosen = iota((groups, LANES), 0) == group
            fields = [high[b : b + 1], low[b : b + 1]]
            fields += [piece[d : d + 1, lanes] for d in range(3) for piece in pieces]
            for index, field in enumerate(fields):
                left[grid, index * groups : (index + 1) * groups, lanes] = jnp.where(
                    chosen, field, 0.0
                ).astype(BF16)
        packed = lax.dot_general(left[grid], right[grid], NT, preferred_element_type=F32)
        part = [packed[i * groups : (i + 1) * groups] for i in range(11)]
        request[:, 4 * grid, :] = part[0] * 256.0 + part[1]
        for d in range(3):
            request[:, 4 * grid + 1 + d, :] = part[2 + 3 * d] + part[3 + 3 * d] + part[4 + 3 * d]
    for edge in (inner_edge, outer_edge):
        edge[layer + blocks :, :] = integers[4].astype(F32)
    for copy in edges:
        copy.wait()


def table_kernel(tile, block, *tables):
    for grid, source in enumerate((tile, block)):
        main, rest = tables[2 * grid : 2 * grid + 2]
        components, rows, depth = source.shape
        for c in range(components):
            for start in range(0, rows, LANES):
                turned = source[c, start : start + LANES, :].T
                coarse = turned.astype(BF16)
                fine = (turned - coarse.astype(F32)) * FINE
                where = slice(c * depth, (c + 1) * depth)
                main[where, start : start + LANES] = coarse
                rest[where, start : start + LANES] = turned.astype(F8)
                rest[where, rows + start : rows + start + LANES] = fine.astype(F8)


def donor_kernel(
    spans, width, request, tile_main, tile_rest, block_main, block_rest, values,
    tile_weights, tile_fines, block_weights, block_fines,
):
    senders = request.shape[0]
    step = width // LANES
    nothing = jnp.zeros((), BF16)
    for first in range(0, senders, step):
        for grid, (main, rest, weights, fines) in enumerate((
            (tile_main, tile_rest, tile_weights, tile_fines),
            (block_main, block_rest, block_weights, block_fines),
        )):
            span_x, span_y, span_z = spans[grid]
            rows = span_x * span_y
            fields = [
                jnp.concatenate(
                    [request[first + s, 4 * grid + f, :][None] for s in range(step)], axis=1
                )
                for f in range(4)
            ]
            base = fields[0].astype(jnp.int32)
            place_z = base % span_z
            row = base // span_z
            place_y = row % span_y
            place_x = row // span_y
            frac_x, frac_y, frac_z = fields[1:]
            along = small_iota((span_y, width), 0)
            lower = along == small(place_y)
            upper = along == small(place_y + 1)
            for x in range(span_x):
                factor = jnp.where(
                    place_x == x, 1.0 - frac_x, jnp.where(place_x == x - 1, frac_x, 0.0)
                )
                coarse = []
                fine = []
                for weight in (factor * (1.0 - frac_y), factor * frac_y):
                    coarse.append(weight.astype(BF16))
                    fine.append(((weight - coarse[-1].astype(F32)) * FINE).astype(BF16))
                main_weight = jnp.where(lower, coarse[0], jnp.where(upper, coarse[1], nothing))
                rest_weight = jnp.where(lower, fine[0], jnp.where(upper, fine[1], nothing))
                here = slice(x * span_y, (x + 1) * span_y)
                weights[here, :] = main_weight
                fines[here, :] = rest_weight.astype(F8)
                fines[rows + x * span_y : rows + (x + 1) * span_y, :] = main_weight.astype(F8)
            mixed = lax.dot_general(main[...], weights[...], NN, preferred_element_type=F32)
            mixed = mixed + (1.0 / FINE) * lax.dot_general(
                rest[...], fines[...], NN, preferred_element_type=F32
            )
            along = iota((span_z, width), 0)
            weight_z = jnp.where(
                along == place_z, 1.0 - frac_z, jnp.where(along == place_z + 1, frac_z, 0.0)
            )
            for c in range(4):
                total = jnp.sum(
                    mixed[c * span_z : (c + 1) * span_z] * weight_z, axis=0, keepdims=True
                )
                for s in range(step):
                    values[first + s, 4 * grid + c, :] = total[0, s * LANES : (s + 1) * LANES]


def mask_kernel(
    block_y, nb_cells, bg_cells, inner, outer,
    nb_hits, bg_hits, inner_hits, outer_hits, nb_taken, bg_taken, inner_taken, outer_taken,
    notes, marks, sems,
):
    blocks, depth = nb_cells.shape[0], LANES
    odd = parity()
    first = inner.shape[0] - blocks
    copies = [
        pltpu.make_async_copy(halo.at[pl.ds(first, blocks)], notes.at[k], sems.at[k])
        for k, halo in enumerate((inner, outer))
    ]
    for copy in copies:
        copy.start()
    one, nothing = jnp.ones((), BF16), jnp.zeros((), BF16)
    span_y = inner_hits.shape[0]
    last = bg_hits.shape[0] // span_y - 1
    sets = (
        (nb_cells, nb_hits, nb_taken, block_y, list(range(nb_hits.shape[0] // block_y))),
        (bg_cells, bg_hits, bg_taken, span_y, list(range(last + 1))),
        (notes.at[0], inner_hits, inner_taken, span_y, [odd * last]),
        (notes.at[1], outer_hits, outer_taken, span_y, [(1 - odd) * last]),
    )
    for k, (cells, hits, taken, rows, planes) in enumerate(sets):
        if k > 1:
            copies[k - 2].wait()
        for b in range(blocks):
            lanes = slice(b * LANES, (b + 1) * LANES)
            cell = cells[b : b + 1, :].astype(jnp.int32)
            z = cell % depth
            row = cell // depth
            y = row % rows
            x = row // rows
            marks[k, :, lanes] = jnp.where(
                small_iota((depth, LANES), 0) == small(z), one, nothing
            ).astype(F8)
            along = small_iota((rows, LANES), 0)
            for index, plane in enumerate(planes):
                hit = small(jnp.where(x == plane, y, -1))
                hits[index * rows : (index + 1) * rows, lanes] = jnp.where(
                    along == hit, one, nothing
                ).astype(F8)
        taken[...] = lax.dot_general(
            hits[...], marks[k], NT, preferred_element_type=F32
        ).astype(BF16)


def receive(k, slots, cells, returned, spots, depth):
    groups = returned.shape[0]
    blocks = slots.shape[0]
    lhs = []
    for c in range(4):
        lhs += split(returned[:, 4 * k + c, :], 2)
    lhs = jnp.concatenate([lhs[2 * c + s] for s in range(2) for c in range(4)], axis=0)
    size = 4 * groups
    one, nothing = jnp.ones((), BF16), jnp.zeros((), BF16)
    for b in range(blocks):
        lanes = slice(b * LANES, (b + 1) * LANES)
        slot = slots[b : b + 1].astype(jnp.int32)
        z = cells[b : b + 1].astype(jnp.int32) % depth
        group = slot >> 7
        place = slot & (LANES - 1)
        along = small_iota((LANES, LANES), 0)
        onehot = jnp.where(along == small(place), one, nothing)
        found = lax.dot_general(lhs, onehot, NN, preferred_element_type=F32)
        found = found[:size] + found[size:]
        chosen = iota((groups, LANES), 0) == group
        mark = along == small(z)
        for c in range(4):
            value = SCALE * jnp.sum(
                jnp.where(chosen, found[c * groups : (c + 1) * groups], 0.0),
                axis=0,
                keepdims=True,
            )
            for s in range(3):
                piece = value.astype(F8).astype(F32)
                value = value - piece
                spots[4 * s + c, :, lanes] = jnp.where(
                    mark, piece.astype(BF16), nothing
                ).astype(F8)


def place_values(hits, taken, spots, old, fields, rows, sources, targets):
    for c in range(0, 4, 2):
        placed = None
        for s in (0, 4, 8):
            pair = spots[s + c : s + c + 2].reshape(2 * LANES, -1)
            part = lax.dot_general(hits[...], pair, NT, preferred_element_type=F32)
            placed = part if placed is None else placed + part
        for index, (source, target) in enumerate(zip(sources, targets)):
            here = slice(index * rows, (index + 1) * rows)
            mask = taken[here, :].astype(F32) > 0.5
            for d in range(2):
                merged = jnp.where(
                    mask, (1.0 / SCALE) * placed[here, d * LANES : (d + 1) * LANES],
                    old[c + d, source],
                )
                fields[c + d, target, 8 : 8 + rows, :] = merged
                fields[c + d, target, 0:8, :] = merged[rows - 8 :]
                fields[c + d, target, 8 + rows :, :] = merged[:8]


def advance(fields, kappa, result, size, offset):
    planes, span_y, depth = kappa.shape
    lane = iota((size, depth), 1)
    count = fields.shape[1]
    for x in range(planes):
        for start in range(0, span_y, size):
            scale = time_step * kappa[x, start : start + size, :]
            middle = slice(8 + start, 8 + start + size)
            speeds = [(-0.5 * time_step) * fields[d, x + offset, middle, :] for d in range(3)]
            for c in range(4):
                here = fields[c, x + offset, middle, :]
                left = fields[c, x + offset, 7 + start : 7 + start + size, :]
                right = fields[c, x + offset, 9 + start : 9 + start + size, :]
                up = jnp.where(lane == depth - 1, 0.0, pltpu.roll(here, depth - 1, 1))
                down = jnp.where(lane == 0, 0.0, pltpu.roll(here, 1, 1))
                total = (left + right) + (up + down) - 6.0 * here
                if x + offset == 0:
                    ahead = fields[c, x + offset + 1, middle, :]
                    total, slope = total + ahead, ahead
                elif x + offset == count - 1:
                    behind = fields[c, x + offset - 1, middle, :]
                    total, slope = total + behind, -behind
                else:
                    behind = fields[c, x + offset - 1, middle, :]
                    ahead = fields[c, x + offset + 1, middle, :]
                    total, slope = total + (behind + ahead), ahead - behind
                result[c, x, start : start + size, :] = (
                    here
                    + scale * total
                    + speeds[0] * slope
                    + speeds[1] * (right - left)
                    + speeds[2] * (up - down)
                )


def finish_kernel(
    returned, slots, nb_cells, bg_cells,
    nb_hits, bg_hits, inner_hits, outer_hits, nb_taken, bg_taken, inner_taken, outer_taken,
    far_inner, far_outer, far_background, far_near_body, far_bg_kappa, far_nb_kappa,
    new_background, new_near_body,
    inner, outer, background, near_body, bg_kappa, nb_kappa, tile_result, block_result,
    tile_fields, block_fields, spots, sems,
):
    blocks, depth = nb_cells.shape[0], bg_kappa.shape[2]
    span_x, span_y = bg_kappa.shape[:2]
    block_x, block_y = nb_kappa.shape[:2]
    components = background.shape[0]
    layer = components * span_y
    odd = parity()
    copies = [
        pltpu.make_async_copy(source, target, sems.at[i])
        for i, (source, target) in enumerate((
            (far_near_body, near_body), (far_background, background), (far_inner, inner),
            (far_outer, outer), (far_nb_kappa, nb_kappa), (far_bg_kappa, bg_kappa),
        ))
    ]
    for copy in copies:
        copy.start()
    receive(0, slots[:blocks, :], nb_cells[...], returned, spots.at[0], depth)
    receive(1, slots[blocks:, :], bg_cells[...], returned, spots.at[1], depth)
    for copy in copies:
        copy.wait()
    place_values(
        nb_hits, nb_taken, spots.at[0], near_body, block_fields, block_y,
        range(block_x), range(block_x),
    )
    place_values(
        bg_hits, bg_taken, spots.at[1], background, tile_fields, span_y,
        range(span_x), range(1, span_x + 1),
    )
    for k, halo in ((2, inner), (3, outer)):
        receive(
            k, halo[layer : layer + blocks, :], halo[layer + blocks :, :],
            returned, spots.at[k], depth,
        )
    advance(block_fields, nb_kappa, block_result, 32, 0)
    sent = pltpu.make_async_copy(block_result, new_near_body, sems.at[6])
    sent.start()
    for k, halo, hits, taken, target in (
        (2, inner, inner_hits, inner_taken, (1 - odd) * (span_x + 1)),
        (3, outer, outer_hits, outer_taken, odd * (span_x + 1)),
    ):
        old = halo[:layer, :].reshape(components, 1, span_y, depth)
        place_values(hits, taken, spots.at[k], old, tile_fields, span_y, [0], [target])
    advance(tile_fields, bg_kappa, tile_result, 32, 1)
    last = pltpu.make_async_copy(tile_result, new_background, sems.at[7])
    last.start()
    sent.wait()
    last.wait()


def call(kernel, outs, scratch, flops, *operands, in_specs=None, out_specs=None):
    moved = sum(a.size * a.dtype.itemsize for a in operands)
    moved += sum(o.size * o.dtype.itemsize for o in outs)
    specs = {}
    if in_specs is not None:
        specs = dict(in_specs=in_specs, out_specs=out_specs)
    return pl.pallas_call(
        kernel,
        out_shape=outs,
        scratch_shapes=scratch,
        compiler_params=pltpu.CompilerParams(vmem_limit_bytes=20 * MIB),
        cost_estimate=pl.CostEstimate(flops=flops, bytes_accessed=moved, transcendentals=0),
        **specs,
    )(*operands)


def distant(array):
    return pltpu.with_memory_space_constraint(array, pltpu.HBM)


def body(
    background, near_body, bg_kappa, nb_kappa,
    nb_recv_cell, nb_donor_owner, nb_donor_base, nb_donor_frac,
    bg_recv_cell, bg_donor_owner, bg_donor_base, bg_donor_frac,
):
    peers = lax.axis_size("tile")
    components, span_x, span_y, depth = background.shape
    block_x, block_y = near_body.shape[1:3]
    receptors = nb_recv_cell.shape[0]
    capacity = 2 * receptors // peers
    blocks = receptors // LANES
    groups = peers * capacity // LANES
    layer = components * span_y
    shape = jax.ShapeDtypeStruct

    def to_peers(array):
        if capacity == LANES:
            return array
        rows = array.shape[1]
        array = array.reshape(groups, rows, LANES // capacity, capacity)
        return array.transpose(0, 2, 1, 3).reshape(peers, rows, capacity)

    def to_groups(array):
        if capacity == LANES:
            return array
        rows = array.shape[1]
        array = array.reshape(groups, LANES // capacity, rows, capacity)
        return array.transpose(0, 2, 1, 3).reshape(groups, rows, LANES)

    def lines(array):
        return array.reshape(blocks, LANES)

    nb_cells, bg_cells = lines(nb_recv_cell), lines(bg_recv_cell)
    far = pl.BlockSpec(memory_space=pltpu.HBM)
    near = pl.BlockSpec(memory_space=pltpu.VMEM)
    request, slots, inner_edge, outer_edge = call(
        functools.partial(pack_kernel, peers, capacity),
        [
            shape((groups, 8, LANES), F32),
            shape((2 * blocks, LANES), F32),
            shape((layer + 2 * blocks, LANES), F32),
            shape((layer + 2 * blocks, LANES), F32),
        ],
        [
            pltpu.VMEM((5, blocks, LANES), jnp.int32),
            pltpu.VMEM((2, 3, receptors), F32),
            pltpu.VMEM((2, 11 * groups, receptors), BF16),
            pltpu.VMEM((2, LANES, receptors), BF16),
            pltpu.SemaphoreType.DMA((7 + 2 * components,)),
        ],
        100_000_000,
        *(
            distant(operand)
            for operand in (
                lines(nb_donor_owner), lines(nb_donor_base), nb_donor_frac, nb_cells,
                lines(bg_donor_owner), lines(bg_donor_base), bg_donor_frac, bg_cells, background,
            )
        ),
        in_specs=[far] * 9,
        out_specs=[near] * 4,
    )
    request = to_groups(lax.all_to_all(to_peers(request), "tile", 0, 0, tiled=True))

    inner_pairs = [(i, i ^ 1) for i in range(peers)]
    outer_pairs = [(i, ((i + 1) ^ 1) - 1) for i in range(1, peers - 1)]
    inner = lax.ppermute(inner_edge, "tile", inner_pairs)
    outer = lax.ppermute(outer_edge, "tile", outer_pairs)

    rows = span_x * span_y
    block_rows = block_x * block_y
    tables = call(
        table_kernel,
        [
            shape((components * depth, rows), BF16),
            shape((components * depth, 2 * rows), F8),
            shape((components * depth, block_rows), BF16),
            shape((components * depth, 2 * block_rows), F8),
        ],
        [],
        1_000_000,
        background.reshape(components, rows, depth),
        near_body.reshape(components, block_rows, depth),
    )
    width = 2 * LANES
    spans = ((span_x, span_y, depth), (block_x, block_y, depth))
    (values,) = call(
        functools.partial(donor_kernel, spans, width),
        [shape((groups, 8, LANES), F32)],
        [
            pltpu.VMEM((rows, width), BF16),
            pltpu.VMEM((2 * rows, width), F8),
            pltpu.VMEM((block_rows, width), BF16),
            pltpu.VMEM((2 * block_rows, width), F8),
        ],
        2_000_000_000,
        request, *tables,
    )
    values = to_peers(values)
    spare = values[:, 4:]
    tail = spare.shape[1:]
    empty = jnp.zeros((1,) + tail, F32)
    from_inner = jnp.flip(spare.reshape((peers // 2, 2) + tail), 1).reshape((peers,) + tail)
    middle = jnp.flip(spare[1:-1].reshape((peers // 2 - 1, 2) + tail), 1)
    from_outer = jnp.concatenate([empty, middle.reshape((peers - 2,) + tail), empty], axis=0)
    response = jnp.concatenate([values, from_inner, from_outer], axis=1)
    returned = to_groups(lax.all_to_all(response, "tile", 0, 0, tiled=True))

    sizes = (block_rows, rows, span_y, span_y)
    found = call(
        functools.partial(mask_kernel, block_y),
        [shape((size, receptors), F8) for size in sizes]
        + [shape((size, LANES), BF16) for size in sizes],
        [
            pltpu.VMEM((2, blocks, LANES), F32),
            pltpu.VMEM((4, depth, receptors), F8),
            pltpu.SemaphoreType.DMA((2,)),
        ],
        1_000_000_000,
        nb_cells, bg_cells, distant(inner), distant(outer),
        in_specs=[near] * 2 + [far] * 2,
        out_specs=[near] * 8,
    )
    edge = (layer + 2 * blocks, LANES)
    return tuple(
        call(
            finish_kernel,
            [shape(background.shape, F32), shape(near_body.shape, F32)],
            [
                pltpu.VMEM(edge, F32),
                pltpu.VMEM(edge, F32),
                pltpu.VMEM(background.shape, F32),
                pltpu.VMEM(near_body.shape, F32),
                pltpu.VMEM(bg_kappa.shape, F32),
                pltpu.VMEM(nb_kappa.shape, F32),
                pltpu.VMEM(background.shape, F32),
                pltpu.VMEM(near_body.shape, F32),
                pltpu.VMEM((components, span_x + 2, span_y + 16, depth), F32),
                pltpu.VMEM((components, block_x, block_y + 16, depth), F32),
                pltpu.VMEM((4, 12, depth, receptors), F8),
                pltpu.SemaphoreType.DMA((8,)),
            ],
            2_000_000_000,
            returned, slots, nb_cells, bg_cells, *found,
            *(
                distant(operand)
                for operand in (inner, outer, background, near_body, bg_kappa, nb_kappa)
            ),
            in_specs=[near] * 12 + [far] * 6,
            out_specs=[far] * 2,
        )
    )


def solution(mesh):
    both = ("group", "tile")
    field = P("group", "tile", None, None)
    row = (P(both), P(both, None), P(both), P(None, both))
    return jax.shard_map(
        body,
        mesh=mesh,
        in_specs=(field, field, P(both, None, None), P(both, None, None)) + row + row,
        out_specs=(field, field),
        check_vma=False,
    )
```

```python
import functools
import math

import jax
import jax.numpy as jnp
from jax import lax
from jax.experimental import pallas as pl
from jax.experimental.pallas import tpu as pltpu
from jax.sharding import PartitionSpec as P

time_step = 0.05
LANES = 128
F32 = jnp.float32
BF16 = jnp.bfloat16
F8 = jnp.float8_e4m3fn
FINE = 512.0
SCALE = 64.0
NT = (((1,), (1,)), ((), ()))
NN = (((1,), (0,)), ((), ()))
MIB = 1024 * 1024


def iota(shape, dim):
    return lax.broadcasted_iota(jnp.int32, shape, dim)


def small_iota(shape, dim):
    return iota(shape, dim).astype(F32).astype(BF16)


def small(value):
    return value.astype(F32).astype(BF16)


def split(value, pieces):
    result = []
    for _ in range(pieces):
        piece = value.astype(BF16)
        result.append(piece)
        value = value - piece.astype(F32)
    return result


def parity():
    return lax.rem(lax.axis_index("tile"), 2)


def pack_kernel(
    peers, capacity, nb_owner, nb_base, nb_frac, bg_owner, bg_base, bg_frac, request, slots,
    integers, fractions, left, right, sems,
):
    blocks = integers.shape[1]
    groups = request.shape[0]
    loads = [
        pltpu.make_async_copy(source, integers.at[i], sems.at[i])
        for i, source in enumerate((nb_owner, nb_base, bg_owner, bg_base))
    ]
    loads += [
        pltpu.make_async_copy(source, fractions.at[i], sems.at[4 + i])
        for i, source in enumerate((nb_frac, bg_frac))
    ]
    for copy in loads:
        copy.start()
    before = iota((LANES, 2 * LANES), 0) < iota((LANES, 2 * LANES), 1)
    triangle = jnp.where(before, 1.0, 0.0).astype(BF16)
    for copy in loads:
        copy.wait()
    for grid in range(2):
        owners = integers[2 * grid]
        hits = [
            jnp.where(iota((peers, LANES), 0) == owners[b : b + 1], 1.0, 0.0)
            for b in range(blocks)
        ]
        counts = lax.dot_general(
            jnp.concatenate(hits, axis=0).astype(BF16), triangle, NN, preferred_element_type=F32
        )
        carry = jnp.zeros((peers, LANES), F32)
        bases = integers[2 * grid + 1]
        high = (bases >> 8).astype(F32)
        low = (bases & 255).astype(F32)
        pieces = []
        rest = fractions[grid]
        for _ in range(3):
            piece = rest.astype(BF16).astype(F32)
            pieces.append(piece)
            rest = rest - piece
        for b in range(blocks):
            rows = slice(b * peers, (b + 1) * peers)
            lanes = slice(b * LANES, (b + 1) * LANES)
            running = counts[rows, :LANES] + carry
            carry = carry + counts[rows, LANES:]
            rank = jnp.sum(hits[b] * running, axis=0, keepdims=True).astype(jnp.int32)
            slot = owners[b : b + 1] * capacity + rank
            slots[grid * blocks + b : grid * blocks + b + 1, :] = slot.astype(F32)
            group = slot >> 7
            place = slot & (LANES - 1)
            right[grid, :, lanes] = jnp.where(
                iota((LANES, LANES), 0) == place, 1.0, 0.0
            ).astype(BF16)
            chosen = iota((groups, LANES), 0) == group
            fields = [high[b : b + 1], low[b : b + 1]]
            fields += [piece[d : d + 1, lanes] for d in range(3) for piece in pieces]
            for index, field in enumerate(fields):
                left[grid, index * groups : (index + 1) * groups, lanes] = jnp.where(
                    chosen, field, 0.0
                ).astype(BF16)
        packed = lax.dot_general(left[grid], right[grid], NT, preferred_element_type=F32)
        part = [packed[i * groups : (i + 1) * groups] for i in range(11)]
        request[:, 4 * grid, :] = part[0] * 256.0 + part[1]
        for d in range(3):
            request[:, 4 * grid + 1 + d, :] = part[2 + 3 * d] + part[3 + 3 * d] + part[4 + 3 * d]


def table_kernel(
    span_y, slots, cells, far_tile, far_block,
    tile_main, tile_rest, block_main, block_rest, inner_edge, outer_edge,
    tile, block, description, sems,
):
    blocks = cells.shape[0]
    copies = [
        pltpu.make_async_copy(source, target, sems.at[i])
        for i, (source, target) in enumerate(((far_tile, tile), (far_block, block)))
    ]
    for copy in copies:
        copy.start()
    description[:blocks, :] = slots[blocks:, :]
    description[blocks:, :] = cells[...].astype(F32)
    odd = parity()
    components, rows, depth = tile.shape
    layer = components * span_y
    sent = []
    for k, (edge, side) in enumerate(((inner_edge, 1 - odd), (outer_edge, odd))):
        sent.append(
            pltpu.make_async_copy(description, edge.at[pl.ds(layer, 2 * blocks)], sems.at[2 + k])
        )
        for c in range(components):
            sent.append(
                pltpu.make_async_copy(
                    tile.at[c, pl.ds(pl.multiple_of(side * (rows - span_y), 8), span_y)],
                    edge.at[pl.ds(c * span_y, span_y)],
                    sems.at[4 + k * components + c],
                )
            )
    copies[0].wait()
    for copy in sent:
        copy.start()
    for source, main, rest in ((tile, tile_main, tile_rest), (block, block_main, block_rest)):
        if source is block:
            copies[1].wait()
        rows = source.shape[1]
        for c in range(components):
            for start in range(0, rows, LANES):
                turned = source[c, start : start + LANES, :].T
                coarse = turned.astype(BF16)
                fine = (turned - coarse.astype(F32)) * FINE
                where = slice(c * depth, (c + 1) * depth)
                main[where, start : start + LANES] = coarse
                rest[where, start : start + LANES] = turned.astype(F8)
                rest[where, rows + start : rows + start + LANES] = fine.astype(F8)
    for copy in sent:
        copy.wait()


def donor_kernel(
    spans, width, shared, request, tile_main, tile_rest, block_main, block_rest, values,
    tile_weights, tile_fines, block_weights, block_fines,
):
    senders = request.shape[0]
    step = width // LANES
    nothing = jnp.zeros((), BF16)
    for first in range(0, senders, step):
        for grid, (main, rest, weights, fines) in enumerate((
            (tile_main, tile_rest, tile_weights, tile_fines),
            (block_main, block_rest, block_weights, block_fines),
        )):
            span_x, span_y, span_z = spans[grid]
            rows = span_x * span_y
            fields = [
                jnp.concatenate(
                    [request[first + s, 4 * grid + f, :][None] for s in range(step)], axis=1
                )
                for f in range(4)
            ]
            base = fields[0].astype(jnp.int32)
            place_z = base % span_z
            row = base // span_z
            place_y = row % span_y
            place_x = row // span_y
            frac_x, frac_y, frac_z = fields[1:]
            along = small_iota((span_y, width), 0)
            lower = along == small(place_y)
            upper = along == small(place_y + 1)
            for x in range(span_x):
                factor = jnp.where(
                    place_x == x, 1.0 - frac_x, jnp.where(place_x == x - 1, frac_x, 0.0)
                )
                coarse = []
                fine = []
                for weight in (factor * (1.0 - frac_y), factor * frac_y):
                    coarse.append(weight.astype(BF16))
                    fine.append(((weight - coarse[-1].astype(F32)) * FINE).astype(BF16))
                main_weight = jnp.where(lower, coarse[0], jnp.where(upper, coarse[1], nothing))
                rest_weight = jnp.where(lower, fine[0], jnp.where(upper, fine[1], nothing))
                here = slice(x * span_y, (x + 1) * span_y)
                weights[here, :] = main_weight
                fines[here, :] = rest_weight.astype(F8)
                fines[rows + x * span_y : rows + (x + 1) * span_y, :] = main_weight.astype(F8)
            mixed = lax.dot_general(main[...], weights[...], NN, preferred_element_type=F32)
            mixed = mixed + (1.0 / FINE) * lax.dot_general(
                rest[...], fines[...], NN, preferred_element_type=F32
            )
            along = iota((span_z, width), 0)
            weight_z = jnp.where(
                along == place_z, 1.0 - frac_z, jnp.where(along == place_z + 1, frac_z, 0.0)
            )
            for c in range(4):
                total = jnp.sum(
                    mixed[c * span_z : (c + 1) * span_z] * weight_z, axis=0, keepdims=True
                )
                for s in range(step):
                    sender = first + s
                    line = total[0, s * LANES : (s + 1) * LANES]
                    values[sender, 4 * grid + c, :] = line
                    if grid and shared:
                        values[sender ^ 1, 8 + c, :] = line
                        if 0 < sender < senders - 1:
                            values[((sender + 1) ^ 1) - 1, 12 + c, :] = line
                        else:
                            values[sender, 12 + c, :] = jnp.zeros((LANES,), F32)


def mask_kernel(
    block_y, nb_cells, bg_cells, inner, outer,
    nb_hits, bg_hits, inner_hits, outer_hits, nb_taken, bg_taken, inner_taken, outer_taken,
    notes, marks, sems,
):
    blocks, depth = nb_cells.shape[0], LANES
    odd = parity()
    first = inner.shape[0] - 2 * blocks
    copies = [
        pltpu.make_async_copy(halo.at[pl.ds(first, 2 * blocks)], notes.at[k], sems.at[k])
        for k, halo in enumerate((inner, outer))
    ]
    for copy in copies:
        copy.start()
    one, nothing = jnp.ones((), BF16), jnp.zeros((), BF16)
    span_y = inner_hits.shape[0]
    last = bg_hits.shape[0] // span_y - 1
    sets = (
        (nb_cells, nb_hits, nb_taken, block_y, list(range(nb_hits.shape[0] // block_y))),
        (bg_cells, bg_hits, bg_taken, span_y, list(range(last + 1))),
        (notes.at[0, pl.ds(blocks, blocks)], inner_hits, inner_taken, span_y, [odd * last]),
        (notes.at[1, pl.ds(blocks, blocks)], outer_hits, outer_taken, span_y, [(1 - odd) * last]),
    )
    for k, (cells, hits, taken, rows, planes) in enumerate(sets):
        if k > 1:
            copies[k - 2].wait()
        for b in range(blocks):
            lanes = slice(b * LANES, (b + 1) * LANES)
            cell = cells[b : b + 1, :].astype(jnp.int32)
            z = cell % depth
            row = cell // depth
            y = row % rows
            x = row // rows
            marks[k, :, lanes] = jnp.where(
                small_iota((depth, LANES), 0) == small(z), one, nothing
            ).astype(F8)
            along = small_iota((rows, LANES), 0)
            for index, plane in enumerate(planes):
                hit = small(jnp.where(x == plane, y, -1))
                hits[index * rows : (index + 1) * rows, lanes] = jnp.where(
                    along == hit, one, nothing
                ).astype(F8)
        taken[...] = lax.dot_general(
            hits[...], marks[k], NT, preferred_element_type=F32
        ).astype(BF16)


def receive(k, slots, cells, returned, spots, depth):
    groups = returned.shape[0]
    blocks = slots.shape[0]
    lhs = []
    for c in range(4):
        lhs += split(returned[:, 4 * k + c, :], 2)
    lhs = jnp.concatenate([lhs[2 * c + s] for s in range(2) for c in range(4)], axis=0)
    size = 4 * groups
    one, nothing = jnp.ones((), BF16), jnp.zeros((), BF16)
    for b in range(blocks):
        lanes = slice(b * LANES, (b + 1) * LANES)
        slot = slots[b : b + 1].astype(jnp.int32)
        z = cells[b : b + 1].astype(jnp.int32) % depth
        group = slot >> 7
        place = slot & (LANES - 1)
        along = small_iota((LANES, LANES), 0)
        onehot = jnp.where(along == small(place), one, nothing)
        found = lax.dot_general(lhs, onehot, NN, preferred_element_type=F32)
        found = found[:size] + found[size:]
        chosen = iota((groups, LANES), 0) == group
        mark = along == small(z)
        for c in range(4):
            value = SCALE * jnp.sum(
                jnp.where(chosen, found[c * groups : (c + 1) * groups], 0.0),
                axis=0,
                keepdims=True,
            )
            for s in range(3):
                piece = value.astype(F8).astype(F32)
                value = value - piece
                spots[4 * s + c, :, lanes] = jnp.where(
                    mark, piece.astype(BF16), nothing
                ).astype(F8)


def place_values(hits, taken, spots, old, fields, rows, sources, targets):
    for c in range(0, 4, 2):
        placed = None
        for s in (0, 4, 8):
            pair = spots[s + c : s + c + 2].reshape(2 * LANES, -1)
            part = lax.dot_general(hits[...], pair, NT, preferred_element_type=F32)
            placed = part if placed is None else placed + part
        for index, (source, target) in enumerate(zip(sources, targets)):
            here = slice(index * rows, (index + 1) * rows)
            mask = taken[here, :].astype(F32) > 0.5
            for d in range(2):
                merged = jnp.where(
                    mask, (1.0 / SCALE) * placed[here, d * LANES : (d + 1) * LANES],
                    old[c + d, source],
                )
                fields[c + d, target, 8 : 8 + rows, :] = merged
                fields[c + d, target, 0:8, :] = merged[rows - 8 :]
                fields[c + d, target, 8 + rows :, :] = merged[:8]


def advance(fields, kappa, result, size, offset):
    for x in range(kappa.shape[0]):
        advance_plane(fields, kappa, result, size, offset, x)


def advance_plane(fields, kappa, result, size, offset, x):
    span_y, depth = kappa.shape[1:]
    lane = iota((size, depth), 1)
    count = fields.shape[1]
    if True:
        for start in range(0, span_y, size):
            scale = time_step * kappa[x, start : start + size, :]
            middle = slice(8 + start, 8 + start + size)
            speeds = [(-0.5 * time_step) * fields[d, x + offset, middle, :] for d in range(3)]
            for c in range(4):
                here = fields[c, x + offset, middle, :]
                left = fields[c, x + offset, 7 + start : 7 + start + size, :]
                right = fields[c, x + offset, 9 + start : 9 + start + size, :]
                up = jnp.where(lane == depth - 1, 0.0, pltpu.roll(here, depth - 1, 1))
                down = jnp.where(lane == 0, 0.0, pltpu.roll(here, 1, 1))
                total = (left + right) + (up + down) - 6.0 * here
                if x + offset == 0:
                    ahead = fields[c, x + offset + 1, middle, :]
                    total, slope = total + ahead, ahead
                elif x + offset == count - 1:
                    behind = fields[c, x + offset - 1, middle, :]
                    total, slope = total + behind, -behind
                else:
                    behind = fields[c, x + offset - 1, middle, :]
                    ahead = fields[c, x + offset + 1, middle, :]
                    total, slope = total + (behind + ahead), ahead - behind
                result[c, x, start : start + size, :] = (
                    here
                    + scale * total
                    + speeds[0] * slope
                    + speeds[1] * (right - left)
                    + speeds[2] * (up - down)
                )


def finish_kernel(
    returned, slots, nb_cells, bg_cells,
    nb_hits, bg_hits, inner_hits, outer_hits, nb_taken, bg_taken, inner_taken, outer_taken, notes,
    far_inner, far_outer, far_background, far_near_body, far_bg_kappa, far_nb_kappa,
    new_background, new_near_body,
    inner, outer, background, near_body, bg_kappa, nb_kappa, tile_result, block_result,
    tile_fields, block_fields, spots, sems,
):
    blocks, depth = nb_cells.shape[0], bg_kappa.shape[2]
    span_x, span_y = bg_kappa.shape[:2]
    block_x, block_y = nb_kappa.shape[:2]
    components = background.shape[0]
    layer = components * span_y
    odd = parity()
    near_copy, nb_copy, tile_copy, inner_copy, outer_copy, bg_copy = copies = [
        pltpu.make_async_copy(source, target, sems.at[i])
        for i, (source, target) in enumerate((
            (far_near_body, near_body), (far_nb_kappa, nb_kappa), (far_background, background),
            (far_inner.at[pl.ds(0, layer)], inner), (far_outer.at[pl.ds(0, layer)], outer),
            (far_bg_kappa, bg_kappa),
        ))
    ]
    for copy in copies:
        copy.start()
    receive(0, slots[:blocks, :], nb_cells[...], returned, spots.at[0], depth)
    receive(1, slots[blocks:, :], bg_cells[...], returned, spots.at[1], depth)
    for k in range(2):
        receive(
            2 + k, notes[k, :blocks, :], notes[k, blocks:, :], returned, spots.at[2 + k], depth
        )
    near_copy.wait()
    place_values(
        nb_hits, nb_taken, spots.at[0], near_body, block_fields, block_y,
        range(block_x), range(block_x),
    )
    tile_copy.wait()
    place_values(
        bg_hits, bg_taken, spots.at[1], background, tile_fields, span_y,
        range(span_x), range(1, span_x + 1),
    )
    nb_copy.wait()
    advance(block_fields, nb_kappa, block_result, 32, 0)
    sent = [pltpu.make_async_copy(block_result, new_near_body, sems.at[6])]
    sent[0].start()
    inner_copy.wait()
    outer_copy.wait()
    for k, halo, hits, taken, target in (
        (2, inner, inner_hits, inner_taken, (1 - odd) * (span_x + 1)),
        (3, outer, outer_hits, outer_taken, odd * (span_x + 1)),
    ):
        old = halo.at[:, :].reshape(components, 1, span_y, depth)
        place_values(hits, taken, spots.at[k], old, tile_fields, span_y, [0], [target])
    bg_copy.wait()
    for x in range(span_x):
        advance_plane(tile_fields, bg_kappa, tile_result, 32, 1, x)
        sent.append(
            pltpu.make_async_copy(tile_result.at[:, x], new_background.at[:, x], sems.at[7 + x])
        )
        sent[-1].start()
    for copy in sent:
        copy.wait()


def call(kernel, outs, scratch, flops, *operands, in_specs=None, out_specs=None):
    moved = sum(a.size * a.dtype.itemsize for a in operands)
    moved += sum(math.prod(o.shape) * jnp.dtype(o.dtype).itemsize for o in outs)
    specs = {}
    if in_specs is not None:
        specs = dict(in_specs=in_specs, out_specs=out_specs)
    return pl.pallas_call(
        kernel,
        out_shape=outs,
        scratch_shapes=scratch,
        compiler_params=pltpu.CompilerParams(vmem_limit_bytes=20 * MIB),
        cost_estimate=pl.CostEstimate(flops=flops, bytes_accessed=moved, transcendentals=0),
        **specs,
    )(*operands)


def distant(array):
    return pltpu.with_memory_space_constraint(array, pltpu.HBM)


def body(
    background, near_body, bg_kappa, nb_kappa,
    nb_recv_cell, nb_donor_owner, nb_donor_base, nb_donor_frac,
    bg_recv_cell, bg_donor_owner, bg_donor_base, bg_donor_frac,
):
    peers = lax.axis_size("tile")
    components, span_x, span_y, depth = background.shape
    block_x, block_y = near_body.shape[1:3]
    receptors = nb_recv_cell.shape[0]
    capacity = 2 * receptors // peers
    blocks = receptors // LANES
    groups = peers * capacity // LANES
    layer = components * span_y
    shape = jax.ShapeDtypeStruct

    def to_peers(array):
        if capacity == LANES:
            return array
        rows = array.shape[1]
        array = array.reshape(groups, rows, LANES // capacity, capacity)
        return array.transpose(0, 2, 1, 3).reshape(peers, rows, capacity)

    def to_groups(array):
        if capacity == LANES:
            return array
        rows = array.shape[1]
        array = array.reshape(groups, LANES // capacity, rows, capacity)
        return array.transpose(0, 2, 1, 3).reshape(groups, rows, LANES)

    def lines(array):
        return array.reshape(blocks, LANES)

    nb_cells, bg_cells = lines(nb_recv_cell), lines(bg_recv_cell)
    far = pl.BlockSpec(memory_space=pltpu.HBM)
    near = pl.BlockSpec(memory_space=pltpu.VMEM)
    request, slots = call(
        functools.partial(pack_kernel, peers, capacity),
        [shape((groups, 8, LANES), F32), shape((2 * blocks, LANES), F32)],
        [
            pltpu.VMEM((4, blocks, LANES), jnp.int32),
            pltpu.VMEM((2, 3, receptors), F32),
            pltpu.VMEM((2, 11 * groups, receptors), BF16),
            pltpu.VMEM((2, LANES, receptors), BF16),
            pltpu.SemaphoreType.DMA((6,)),
        ],
        100_000_000,
        *(
            distant(operand)
            for operand in (
                lines(nb_donor_owner), lines(nb_donor_base), nb_donor_frac,
                lines(bg_donor_owner), lines(bg_donor_base), bg_donor_frac,
            )
        ),
        in_specs=[far] * 6,
        out_specs=[near] * 2,
    )
    request = to_groups(lax.all_to_all(to_peers(request), "tile", 0, 0, tiled=True))

    rows = span_x * span_y
    block_rows = block_x * block_y
    edge = (layer + 2 * blocks, LANES)
    *tables, inner_edge, outer_edge = call(
        functools.partial(table_kernel, span_y),
        [
            shape((components * depth, rows), BF16),
            shape((components * depth, 2 * rows), F8),
            shape((components * depth, block_rows), BF16),
            shape((components * depth, 2 * block_rows), F8),
            pltpu.HBM(edge, F32),
            pltpu.HBM(edge, F32),
        ],
        [
            pltpu.VMEM((components, rows, depth), F32),
            pltpu.VMEM((components, block_rows, depth), F32),
            pltpu.VMEM((2 * blocks, LANES), F32),
            pltpu.SemaphoreType.DMA((4 + 2 * components,)),
        ],
        1_000_000,
        slots, bg_cells,
        distant(background.reshape(components, rows, depth)),
        distant(near_body.reshape(components, block_rows, depth)),
        in_specs=[near] * 2 + [far] * 2,
        out_specs=[near] * 4 + [far] * 2,
    )
    inner_pairs = [(i, i ^ 1) for i in range(peers)]
    outer_pairs = [(i, ((i + 1) ^ 1) - 1) for i in range(1, peers - 1)]
    inner = lax.ppermute(inner_edge, "tile", inner_pairs)
    outer = lax.ppermute(outer_edge, "tile", outer_pairs)
    width = 2 * LANES
    spans = ((span_x, span_y, depth), (block_x, block_y, depth))
    shared = capacity == LANES
    (values,) = call(
        functools.partial(donor_kernel, spans, width, shared),
        [shape((groups, 16 if shared else 8, LANES), F32)],
        [
            pltpu.VMEM((rows, width), BF16),
            pltpu.VMEM((2 * rows, width), F8),
            pltpu.VMEM((block_rows, width), BF16),
            pltpu.VMEM((2 * block_rows, width), F8),
        ],
        20_000_000_000,
        request, *tables,
    )
    if not shared:
        values = to_peers(values)
        spare = values[:, 4:]
        tail = spare.shape[1:]
        empty = jnp.zeros((1,) + tail, F32)
        from_inner = jnp.flip(spare.reshape((peers // 2, 2) + tail), 1).reshape((peers,) + tail)
        middle = jnp.flip(spare[1:-1].reshape((peers // 2 - 1, 2) + tail), 1)
        from_outer = jnp.concatenate([empty, middle.reshape((peers - 2,) + tail), empty], axis=0)
        values = jnp.concatenate([values, from_inner, from_outer], axis=1)
    returned = to_groups(lax.all_to_all(values, "tile", 0, 0, tiled=True))

    sizes = (block_rows, rows, span_y, span_y)
    found = call(
        functools.partial(mask_kernel, block_y),
        [shape((size, receptors), F8) for size in sizes]
        + [shape((size, LANES), BF16) for size in sizes]
        + [shape((2, 2 * blocks, LANES), F32)],
        [
            pltpu.VMEM((4, depth, receptors), F8),
            pltpu.SemaphoreType.DMA((2,)),
        ],
        1_000_000_000,
        nb_cells, bg_cells, distant(inner), distant(outer),
        in_specs=[near] * 2 + [far] * 2,
        out_specs=[near] * 9,
    )
    return tuple(
        call(
            finish_kernel,
            [shape(background.shape, F32), shape(near_body.shape, F32)],
            [
                pltpu.VMEM((layer, LANES), F32),
                pltpu.VMEM((layer, LANES), F32),
                pltpu.VMEM(background.shape, F32),
                pltpu.VMEM(near_body.shape, F32),
                pltpu.VMEM(bg_kappa.shape, F32),
                pltpu.VMEM(nb_kappa.shape, F32),
                pltpu.VMEM(background.shape, F32),
                pltpu.VMEM(near_body.shape, F32),
                pltpu.VMEM((components, span_x + 2, span_y + 16, depth), F32),
                pltpu.VMEM((components, block_x, block_y + 16, depth), F32),
                pltpu.VMEM((4, 12, depth, receptors), F8),
                pltpu.SemaphoreType.DMA((7 + span_x,)),
            ],
            2_000_000_000,
            returned, slots, nb_cells, bg_cells, *found,
            *(
                distant(operand)
                for operand in (inner, outer, background, near_body, bg_kappa, nb_kappa)
            ),
            in_specs=[near] * 13 + [far] * 6,
            out_specs=[far] * 2,
        )
    )


def solution(mesh):
    both = ("group", "tile")
    field = P("group", "tile", None, None)
    row = (P(both), P(both, None), P(both), P(None, both))
    return jax.shard_map(
        body,
        mesh=mesh,
        in_specs=(field, field, P(both, None, None), P(both, None, None)) + row + row,
        out_specs=(field, field),
        check_vma=False,
    )
```

```python
import functools
import math

import jax
import jax.numpy as jnp
from jax import lax
from jax.experimental import pallas as pl
from jax.experimental.pallas import tpu as pltpu
from jax.sharding import PartitionSpec as P

time_step = 0.05
LANES = 128
F32 = jnp.float32
BF16 = jnp.bfloat16
F8 = jnp.float8_e4m3fn
FINE = 512.0
SCALE = 64.0
NT = (((1,), (1,)), ((), ()))
NN = (((1,), (0,)), ((), ()))
MIB = 1024 * 1024


def iota(shape, dim):
    return lax.broadcasted_iota(jnp.int32, shape, dim)


def small_iota(shape, dim):
    return iota(shape, dim).astype(F32).astype(BF16)


def small(value):
    return value.astype(F32).astype(BF16)


def split(value, pieces):
    result = []
    for _ in range(pieces):
        piece = value.astype(BF16)
        result.append(piece)
        value = value - piece.astype(F32)
    return result


def parity():
    return lax.rem(lax.axis_index("tile"), 2)


def pack_kernel(
    peers, capacity, nb_owner, nb_base, nb_frac, bg_owner, bg_base, bg_frac,
    nb_cell, bg_cell, far_tile, request, slots, nb_cells, bg_cells, tile,
    integers, fractions, left, right, sems,
):
    blocks = integers.shape[1]
    groups = request.shape[0]
    loads = [
        pltpu.make_async_copy(source, target, sems.at[i])
        for i, (source, target) in enumerate((
            (nb_owner, integers.at[0]), (nb_base, integers.at[1]), (nb_frac, fractions.at[0]),
            (bg_owner, integers.at[2]), (bg_base, integers.at[3]), (bg_frac, fractions.at[1]),
            (bg_cell, bg_cells), (nb_cell, nb_cells), (far_tile, tile),
        ))
    ]
    for copy in loads:
        copy.start()
    before = iota((LANES, 2 * LANES), 0) < iota((LANES, 2 * LANES), 1)
    triangle = jnp.where(before, 1.0, 0.0).astype(BF16)
    for copy in loads[:8]:
        copy.wait()
    one, nothing = jnp.ones((), BF16), jnp.zeros((), BF16)
    for grid in range(2):
        owners = integers[2 * grid]
        hits = [
            jnp.where(iota((peers, LANES), 0) == owners[b : b + 1], 1.0, 0.0)
            for b in range(blocks)
        ]
        counts = lax.dot_general(
            jnp.concatenate(hits, axis=0).astype(BF16), triangle, NN, preferred_element_type=F32
        )
        carry = jnp.zeros((peers, LANES), F32)
        bases = integers[2 * grid + 1]
        high = (bases >> 8).astype(F32)
        low = (bases & 255).astype(F32)
        pieces = []
        rest = fractions[grid]
        for _ in range(3):
            piece = rest.astype(BF16).astype(F32)
            pieces.append(piece)
            rest = rest - piece
        for b in range(blocks):
            part = slice(b * peers, (b + 1) * peers)
            lanes = slice(b * LANES, (b + 1) * LANES)
            running = counts[part, :LANES] + carry
            carry = carry + counts[part, LANES:]
            rank = jnp.sum(hits[b] * running, axis=0, keepdims=True).astype(jnp.int32)
            slot = owners[b : b + 1] * capacity + rank
            slots[grid * blocks + b : grid * blocks + b + 1, :] = slot.astype(F32)
            group = slot >> 7
            place = slot & (LANES - 1)
            right[grid, :, lanes] = jnp.where(
                small_iota((LANES, LANES), 0) == small(place), one, nothing
            )
            chosen = iota((groups, LANES), 0) == group
            fields = [high[b : b + 1], low[b : b + 1]]
            fields += [piece[d : d + 1, lanes] for d in range(3) for piece in pieces]
            for index, field in enumerate(fields):
                left[grid, index * groups : (index + 1) * groups, lanes] = jnp.where(
                    chosen, field, 0.0
                ).astype(BF16)
        packed = lax.dot_general(left[grid], right[grid], NT, preferred_element_type=F32)
        part = [packed[i * groups : (i + 1) * groups] for i in range(11)]
        request[:, 4 * grid, :] = part[0] * 256.0 + part[1]
        for d in range(3):
            request[:, 4 * grid + 1 + d, :] = part[2 + 3 * d] + part[3 + 3 * d] + part[4 + 3 * d]
    loads[8].wait()


def table_kernel(
    span_y, slots, cells, tile, far_block,
    tile_main, tile_rest, block_main, block_rest, inner_edge, outer_edge,
    block, description, sems,
):
    blocks = cells.shape[0]
    load = pltpu.make_async_copy(far_block, block, sems.at[0])
    load.start()
    description[:blocks, :] = slots[blocks:, :]
    description[blocks:, :] = cells[...].astype(F32)
    odd = parity()
    components, rows, depth = tile.shape
    layer = components * span_y
    sent = []
    for k, (edge, side) in enumerate(((inner_edge, 1 - odd), (outer_edge, odd))):
        sent.append(
            pltpu.make_async_copy(description, edge.at[pl.ds(layer, 2 * blocks)], sems.at[1 + k])
        )
        for c in range(components):
            sent.append(
                pltpu.make_async_copy(
                    tile.at[c, pl.ds(pl.multiple_of(side * (rows - span_y), 8), span_y)],
                    edge.at[pl.ds(c * span_y, span_y)],
                    sems.at[3 + k * components + c],
                )
            )
    for copy in sent:
        copy.start()
    for source, main, rest in ((tile, tile_main, tile_rest), (block, block_main, block_rest)):
        if source is block:
            load.wait()
        rows = source.shape[1]
        for c in range(components):
            for start in range(0, rows, LANES):
                turned = source[c, start : start + LANES, :].T
                coarse = turned.astype(BF16)
                fine = (turned - coarse.astype(F32)) * FINE
                where = slice(c * depth, (c + 1) * depth)
                main[where, start : start + LANES] = coarse
                rest[where, start : start + LANES] = fine.astype(F8)
    for copy in sent:
        copy.wait()


def mark_cells(cells, hits, marks, span, planes, b):
    one, nothing = jnp.ones((), BF16), jnp.zeros((), BF16)
    lanes = slice(b * LANES, (b + 1) * LANES)
    cell = cells.astype(jnp.int32)
    z = cell % LANES
    row = cell // LANES
    y = row % span
    x = row // span
    marks[:, lanes] = jnp.where(small_iota((LANES, LANES), 0) == small(z), one, nothing).astype(F8)
    along = small_iota((span, LANES), 0)
    for index, plane in enumerate(planes):
        hit = small(jnp.where(x == plane, y, -1))
        hits[index * span : (index + 1) * span, lanes] = jnp.where(
            along == hit, one, nothing
        ).astype(F8)


def taken_of(hits, marks):
    return lax.dot_general(hits[...], marks[...], NT, preferred_element_type=F32).astype(BF16)


def donor_kernel(
    spans, width, shared, nb_cells, bg_cells, request,
    tile_main, tile_rest, block_main, block_rest,
    values, nb_hits, bg_hits, nb_taken, bg_taken,
    tile_weights, tile_fines, tile_rough, block_weights, block_fines, block_rough, marks,
):
    senders = request.shape[0]
    step = width // LANES
    nothing = jnp.zeros((), BF16)
    blocks = nb_cells.shape[0]
    rounds = senders // step
    sets = (
        (nb_cells, nb_hits, marks.at[0], spans[1][1], range(spans[1][0])),
        (bg_cells, bg_hits, marks.at[1], spans[0][1], range(spans[0][0])),
    )
    for first in range(0, senders, step):
        for b in range(first // step * blocks // rounds, (first // step + 1) * blocks // rounds):
            for cells, hits, mark, span, planes in sets:
                mark_cells(cells[b : b + 1, :], hits, mark, span, planes, b)
        for grid, (main, rest, rough, weights, fines) in enumerate((
            (tile_main, tile_rest, tile_rough, tile_weights, tile_fines),
            (block_main, block_rest, block_rough, block_weights, block_fines),
        )):
            if first == 0:
                rough[...] = main[...].astype(F8)
            span_x, span_y, span_z = spans[grid]
            rows = span_x * span_y
            fields = [
                jnp.concatenate(
                    [request[first + s, 4 * grid + f, :][None] for s in range(step)], axis=1
                )
                for f in range(4)
            ]
            base = fields[0].astype(jnp.int32)
            place_z = base % span_z
            row = base // span_z
            place_y = row % span_y
            place_x = row // span_y
            frac_x, frac_y, frac_z = fields[1:]
            along = small_iota((span_y, width), 0)
            lower = along == small(place_y)
            upper = along == small(place_y + 1)
            for x in range(span_x):
                factor = jnp.where(
                    place_x == x, 1.0 - frac_x, jnp.where(place_x == x - 1, frac_x, 0.0)
                )
                coarse = []
                fine = []
                for weight in (factor * (1.0 - frac_y), factor * frac_y):
                    coarse.append(weight.astype(BF16))
                    fine.append(((weight - coarse[-1].astype(F32)) * FINE).astype(BF16))
                main_weight = jnp.where(lower, coarse[0], jnp.where(upper, coarse[1], nothing))
                rest_weight = jnp.where(lower, fine[0], jnp.where(upper, fine[1], nothing))
                here = slice(x * span_y, (x + 1) * span_y)
                weights[here, :] = main_weight
                fines[here, :] = rest_weight.astype(F8)
                fines[rows + x * span_y : rows + (x + 1) * span_y, :] = main_weight.astype(F8)
            mixed = lax.dot_general(main[...], weights[...], NN, preferred_element_type=F32)
            extra = lax.dot_general(
                rough[...], fines[:rows, :], NN, preferred_element_type=F32
            ) + lax.dot_general(rest[...], fines[rows:, :], NN, preferred_element_type=F32)
            mixed = mixed + (1.0 / FINE) * extra
            along = iota((span_z, width), 0)
            weight_z = jnp.where(
                along == place_z, 1.0 - frac_z, jnp.where(along == place_z + 1, frac_z, 0.0)
            )
            for c in range(4):
                total = jnp.sum(
                    mixed[c * span_z : (c + 1) * span_z] * weight_z, axis=0, keepdims=True
                )
                for s in range(step):
                    sender = first + s
                    line = total[0, s * LANES : (s + 1) * LANES]
                    values[sender, 4 * grid + c, :] = line
                    if grid and shared:
                        values[sender ^ 1, 8 + c, :] = line
                        if 0 < sender < senders - 1:
                            values[((sender + 1) ^ 1) - 1, 12 + c, :] = line
                        else:
                            values[sender, 12 + c, :] = jnp.zeros((LANES,), F32)
    nb_taken[...] = taken_of(nb_hits, marks.at[0])
    bg_taken[...] = taken_of(bg_hits, marks.at[1])


def receive(k, slots, cells, returned, spots, depth):
    groups = returned.shape[0]
    blocks = slots.shape[0]
    lhs = []
    for c in range(4):
        lhs += split(returned[:, 4 * k + c, :], 2)
    lhs = jnp.concatenate([lhs[2 * c + s] for s in range(2) for c in range(4)], axis=0)
    size = 4 * groups
    one, nothing = jnp.ones((), BF16), jnp.zeros((), BF16)
    for b in range(blocks):
        lanes = slice(b * LANES, (b + 1) * LANES)
        slot = slots[b : b + 1].astype(jnp.int32)
        z = cells[b : b + 1].astype(jnp.int32) % depth
        group = slot >> 7
        place = slot & (LANES - 1)
        along = small_iota((LANES, LANES), 0)
        onehot = jnp.where(along == small(place), one, nothing)
        found = lax.dot_general(lhs, onehot, NN, preferred_element_type=F32)
        found = found[:size] + found[size:]
        chosen = iota((groups, LANES), 0) == group
        mark = along == small(z)
        for c in range(4):
            value = SCALE * jnp.sum(
                jnp.where(chosen, found[c * groups : (c + 1) * groups], 0.0),
                axis=0,
                keepdims=True,
            )
            for s in range(3):
                piece = value.astype(F8).astype(F32)
                value = value - piece
                spots[4 * s + c, :, lanes] = jnp.where(
                    mark, piece.astype(BF16), nothing
                ).astype(F8)


def place_values(hits, taken, spots, old, fields, rows, sources, targets):
    for c in range(0, 4, 2):
        placed = None
        for s in (0, 4, 8):
            pair = spots[s + c : s + c + 2].reshape(2 * LANES, -1)
            part = lax.dot_general(hits[...], pair, NT, preferred_element_type=F32)
            placed = part if placed is None else placed + part
        for index, (source, target) in enumerate(zip(sources, targets)):
            here = slice(index * rows, (index + 1) * rows)
            mask = taken[here, :].astype(F32) > 0.5
            for d in range(2):
                merged = jnp.where(
                    mask, (1.0 / SCALE) * placed[here, d * LANES : (d + 1) * LANES],
                    old[c + d, source],
                )
                fields[c + d, target, 8 : 8 + rows, :] = merged
                fields[c + d, target, 0:8, :] = merged[rows - 8 :]
                fields[c + d, target, 8 + rows :, :] = merged[:8]


def advance(fields, kappa, result, size, offset):
    for x in range(kappa.shape[0]):
        advance_plane(fields, kappa, result, size, offset, x)


def advance_plane(fields, kappa, result, size, offset, x):
    span_y, depth = kappa.shape[1:]
    lane = iota((size, depth), 1)
    count = fields.shape[1]
    if True:
        for start in range(0, span_y, size):
            scale = time_step * kappa[x, start : start + size, :]
            middle = slice(8 + start, 8 + start + size)
            speeds = [(-0.5 * time_step) * fields[d, x + offset, middle, :] for d in range(3)]
            for c in range(4):
                here = fields[c, x + offset, middle, :]
                left = fields[c, x + offset, 7 + start : 7 + start + size, :]
                right = fields[c, x + offset, 9 + start : 9 + start + size, :]
                up = jnp.where(lane == depth - 1, 0.0, pltpu.roll(here, depth - 1, 1))
                down = jnp.where(lane == 0, 0.0, pltpu.roll(here, 1, 1))
                total = (left + right) + (up + down) - 6.0 * here
                if x + offset == 0:
                    ahead = fields[c, x + offset + 1, middle, :]
                    total, slope = total + ahead, ahead
                elif x + offset == count - 1:
                    behind = fields[c, x + offset - 1, middle, :]
                    total, slope = total + behind, -behind
                else:
                    behind = fields[c, x + offset - 1, middle, :]
                    ahead = fields[c, x + offset + 1, middle, :]
                    total, slope = total + (behind + ahead), ahead - behind
                result[c, x, start : start + size, :] = (
                    here
                    + scale * total
                    + speeds[0] * slope
                    + speeds[1] * (right - left)
                    + speeds[2] * (up - down)
                )


def finish_kernel(
    returned, slots, nb_cells, bg_cells, nb_hits, bg_hits, nb_taken, bg_taken,
    inner, outer, background, near_body, bg_kappa, nb_kappa,
    new_background, new_near_body,
    tile_result, block_result, tile_fields, block_fields, spots, halo_hits, halo_taken, marks,
    sems,
):
    blocks, depth = nb_cells.shape[0], bg_kappa.shape[2]
    span_x, span_y = bg_kappa.shape[:2]
    block_x, block_y = nb_kappa.shape[:2]
    components = background.shape[0]
    layer = components * span_y
    odd = parity()
    receive(0, slots[:blocks, :], nb_cells[...], returned, spots.at[0], depth)
    receive(1, slots[blocks:, :], bg_cells[...], returned, spots.at[1], depth)
    for k, halo in ((2, inner), (3, outer)):
        receive(
            k, halo[layer : layer + blocks, :], halo[layer + blocks :, :], returned,
            spots.at[k], depth,
        )
    for k, (halo, plane) in enumerate(
        ((inner, odd * (span_x - 1)), (outer, (1 - odd) * (span_x - 1)))
    ):
        for b in range(blocks):
            cells = halo[layer + blocks + b : layer + blocks + b + 1, :]
            mark_cells(cells, halo_hits.at[k], marks.at[k], span_y, [plane], b)
        halo_taken[k] = taken_of(halo_hits.at[k], marks.at[k])
    place_values(
        nb_hits, nb_taken, spots.at[0], near_body, block_fields, block_y,
        range(block_x), range(block_x),
    )
    place_values(
        bg_hits, bg_taken, spots.at[1], background, tile_fields, span_y,
        range(span_x), range(1, span_x + 1),
    )
    advance(block_fields, nb_kappa, block_result, 32, 0)
    sent = [pltpu.make_async_copy(block_result, new_near_body, sems.at[0])]
    sent[0].start()
    for k, halo, target in (
        (0, inner, (1 - odd) * (span_x + 1)), (1, outer, odd * (span_x + 1)),
    ):
        old = halo.at[:layer, :].reshape(components, 1, span_y, depth)
        place_values(
            halo_hits.at[k], halo_taken.at[k], spots.at[2 + k], old, tile_fields, span_y,
            [0], [target],
        )
    for x in range(span_x):
        advance_plane(tile_fields, bg_kappa, tile_result, 32, 1, x)
        sent.append(
            pltpu.make_async_copy(tile_result.at[:, x], new_background.at[:, x], sems.at[1 + x])
        )
        sent[-1].start()
    for copy in sent:
        copy.wait()


def call(kernel, outs, scratch, flops, *operands, in_specs=None, out_specs=None):
    moved = sum(a.size * a.dtype.itemsize for a in operands)
    moved += sum(math.prod(o.shape) * jnp.dtype(o.dtype).itemsize for o in outs)
    specs = {}
    if in_specs is not None:
        specs = dict(in_specs=in_specs, out_specs=out_specs)
    return pl.pallas_call(
        kernel,
        out_shape=outs,
        scratch_shapes=scratch,
        compiler_params=pltpu.CompilerParams(vmem_limit_bytes=20 * MIB),
        cost_estimate=pl.CostEstimate(flops=flops, bytes_accessed=moved, transcendentals=0),
        **specs,
    )(*operands)


def distant(array):
    return pltpu.with_memory_space_constraint(array, pltpu.HBM)


def body(
    background, near_body, bg_kappa, nb_kappa,
    nb_recv_cell, nb_donor_owner, nb_donor_base, nb_donor_frac,
    bg_recv_cell, bg_donor_owner, bg_donor_base, bg_donor_frac,
):
    peers = lax.axis_size("tile")
    components, span_x, span_y, depth = background.shape
    block_x, block_y = near_body.shape[1:3]
    receptors = nb_recv_cell.shape[0]
    capacity = 2 * receptors // peers
    blocks = receptors // LANES
    groups = peers * capacity // LANES
    layer = components * span_y
    shape = jax.ShapeDtypeStruct

    def to_peers(array):
        if capacity == LANES:
            return array
        rows = array.shape[1]
        array = array.reshape(groups, rows, LANES // capacity, capacity)
        return array.transpose(0, 2, 1, 3).reshape(peers, rows, capacity)

    def to_groups(array):
        if capacity == LANES:
            return array
        rows = array.shape[1]
        array = array.reshape(groups, LANES // capacity, rows, capacity)
        return array.transpose(0, 2, 1, 3).reshape(groups, rows, LANES)

    def lines(array):
        return array.reshape(blocks, LANES)

    far = pl.BlockSpec(memory_space=pltpu.HBM)
    near = pl.BlockSpec(memory_space=pltpu.VMEM)
    rows = span_x * span_y
    block_rows = block_x * block_y
    edge = (layer + 2 * blocks, LANES)
    request, slots, nb_cells, bg_cells, tile = call(
        functools.partial(pack_kernel, peers, capacity),
        [
            shape((groups, 8, LANES), F32),
            shape((2 * blocks, LANES), F32),
            shape((blocks, LANES), jnp.int32),
            shape((blocks, LANES), jnp.int32),
            shape((components, rows, depth), F32),
        ],
        [
            pltpu.VMEM((4, blocks, LANES), jnp.int32),
            pltpu.VMEM((2, 3, receptors), F32),
            pltpu.VMEM((2, 11 * groups, receptors), BF16),
            pltpu.VMEM((2, LANES, receptors), BF16),
            pltpu.SemaphoreType.DMA((9,)),
        ],
        100_000_000,
        *(
            distant(operand)
            for operand in (
                lines(nb_donor_owner), lines(nb_donor_base), nb_donor_frac,
                lines(bg_donor_owner), lines(bg_donor_base), bg_donor_frac,
                lines(nb_recv_cell), lines(bg_recv_cell),
                background.reshape(components, rows, depth),
            )
        ),
        in_specs=[far] * 9,
        out_specs=[near] * 5,
    )
    request = to_groups(lax.all_to_all(to_peers(request), "tile", 0, 0, tiled=True))
    *tables, inner_edge, outer_edge = call(
        functools.partial(table_kernel, span_y),
        [
            shape((components * depth, rows), BF16),
            shape((components * depth, rows), F8),
            shape((components * depth, block_rows), BF16),
            shape((components * depth, block_rows), F8),
            pltpu.HBM(edge, F32),
            pltpu.HBM(edge, F32),
        ],
        [
            pltpu.VMEM((components, block_rows, depth), F32),
            pltpu.VMEM((2 * blocks, LANES), F32),
            pltpu.SemaphoreType.DMA((3 + 2 * components,)),
        ],
        1_000_000,
        slots, bg_cells, tile, distant(near_body.reshape(components, block_rows, depth)),
        in_specs=[near] * 3 + [far],
        out_specs=[near] * 4 + [far] * 2,
    )
    inner_pairs = [(i, i ^ 1) for i in range(peers)]
    outer_pairs = [(i, ((i + 1) ^ 1) - 1) for i in range(1, peers - 1)]
    inner = lax.ppermute(inner_edge, "tile", inner_pairs)
    outer = lax.ppermute(outer_edge, "tile", outer_pairs)
    width = 2 * LANES
    spans = ((span_x, span_y, depth), (block_x, block_y, depth))
    shared = capacity == LANES
    values, *found = call(
        functools.partial(donor_kernel, spans, width, shared),
        [
            shape((groups, 16 if shared else 8, LANES), F32),
            shape((block_rows, receptors), F8),
            shape((rows, receptors), F8),
            shape((block_rows, LANES), BF16),
            shape((rows, LANES), BF16),
        ],
        [
            pltpu.VMEM((rows, width), BF16),
            pltpu.VMEM((2 * rows, width), F8),
            pltpu.VMEM((components * depth, rows), F8),
            pltpu.VMEM((block_rows, width), BF16),
            pltpu.VMEM((2 * block_rows, width), F8),
            pltpu.VMEM((components * depth, block_rows), F8),
            pltpu.VMEM((2, depth, receptors), F8),
        ],
        20_000_000_000,
        nb_cells, bg_cells, request, *tables,
    )
    if not shared:
        values = to_peers(values)
        spare = values[:, 4:]
        tail = spare.shape[1:]
        empty = jnp.zeros((1,) + tail, F32)
        from_inner = jnp.flip(spare.reshape((peers // 2, 2) + tail), 1).reshape((peers,) + tail)
        middle = jnp.flip(spare[1:-1].reshape((peers // 2 - 1, 2) + tail), 1)
        from_outer = jnp.concatenate([empty, middle.reshape((peers - 2,) + tail), empty], axis=0)
        values = jnp.concatenate([values, from_inner, from_outer], axis=1)
    returned = to_groups(lax.all_to_all(values, "tile", 0, 0, tiled=True))

    return tuple(
        call(
            finish_kernel,
            [shape(background.shape, F32), shape(near_body.shape, F32)],
            [
                pltpu.VMEM(background.shape, F32),
                pltpu.VMEM(near_body.shape, F32),
                pltpu.VMEM((components, span_x + 2, span_y + 16, depth), F32),
                pltpu.VMEM((components, block_x, block_y + 16, depth), F32),
                pltpu.VMEM((4, 12, depth, receptors), F8),
                pltpu.VMEM((2, span_y, receptors), F8),
                pltpu.VMEM((2, span_y, LANES), BF16),
                pltpu.VMEM((2, depth, receptors), F8),
                pltpu.SemaphoreType.DMA((1 + span_x,)),
            ],
            2_000_000_000,
            returned, slots, nb_cells, bg_cells, *found, inner, outer,
            background, near_body, bg_kappa, nb_kappa,
            in_specs=[near] * 14,
            out_specs=[far] * 2,
        )
    )


def solution(mesh):
    both = ("group", "tile")
    field = P("group", "tile", None, None)
    row = (P(both), P(both, None), P(both), P(None, both))
    return jax.shard_map(
        body,
        mesh=mesh,
        in_specs=(field, field, P(both, None, None), P(both, None, None)) + row + row,
        out_specs=(field, field),
        check_vma=False,
    )
```

```python
import functools
import math

import jax
import jax.numpy as jnp
from jax import lax
from jax.experimental import pallas as pl
from jax.experimental.pallas import tpu as pltpu
from jax.sharding import PartitionSpec as P

time_step = 0.05
LANES = 128
F32 = jnp.float32
BF16 = jnp.bfloat16
F8 = jnp.float8_e4m3fn
FINE = 512.0
SCALE = 64.0
NT = (((1,), (1,)), ((), ()))
NN = (((1,), (0,)), ((), ()))
MIB = 1024 * 1024


def iota(shape, dim):
    return lax.broadcasted_iota(jnp.int32, shape, dim)


def small_iota(shape, dim):
    return iota(shape, dim).astype(F32).astype(BF16)


def small(value):
    return value.astype(F32).astype(BF16)


def split(value, pieces):
    result = []
    for _ in range(pieces):
        piece = value.astype(BF16)
        result.append(piece)
        value = value - piece.astype(F32)
    return result


def parity():
    return lax.rem(lax.axis_index("tile"), 2)


def pack_kernel(
    peers, capacity, nb_owner, nb_base, nb_frac, bg_owner, bg_base, bg_frac,
    nb_cell, bg_cell, far_tile, request, slots, nb_cells, bg_cells, tile,
    integers, fractions, left, right, sems,
):
    blocks = integers.shape[1]
    groups = request.shape[0]
    loads = [
        pltpu.make_async_copy(source, target, sems.at[i])
        for i, (source, target) in enumerate((
            (nb_owner, integers.at[0]), (nb_base, integers.at[1]), (nb_frac, fractions.at[0]),
            (bg_owner, integers.at[2]), (bg_base, integers.at[3]), (bg_frac, fractions.at[1]),
            (bg_cell, bg_cells), (nb_cell, nb_cells), (far_tile, tile),
        ))
    ]
    for copy in loads:
        copy.start()
    before = iota((LANES, 2 * LANES), 0) < iota((LANES, 2 * LANES), 1)
    triangle = jnp.where(before, 1.0, 0.0).astype(BF16)
    for copy in loads[:6]:
        copy.wait()
    one, nothing = jnp.ones((), BF16), jnp.zeros((), BF16)
    for grid in range(2):
        owners = integers[2 * grid]
        hits = [
            jnp.where(iota((peers, LANES), 0) == owners[b : b + 1], 1.0, 0.0)
            for b in range(blocks)
        ]
        counts = lax.dot_general(
            jnp.concatenate(hits, axis=0).astype(BF16), triangle, NN, preferred_element_type=F32
        )
        carry = jnp.zeros((peers, LANES), F32)
        bases = integers[2 * grid + 1]
        high = (bases >> 8).astype(F32)
        low = (bases & 255).astype(F32)
        pieces = []
        rest = fractions[grid]
        for _ in range(2):
            piece = rest.astype(BF16).astype(F32)
            pieces.append(piece)
            rest = rest - piece
        for b in range(blocks):
            part = slice(b * peers, (b + 1) * peers)
            lanes = slice(b * LANES, (b + 1) * LANES)
            running = counts[part, :LANES] + carry
            carry = carry + counts[part, LANES:]
            rank = jnp.sum(hits[b] * running, axis=0, keepdims=True).astype(jnp.int32)
            slot = owners[b : b + 1] * capacity + rank
            slots[grid * blocks + b : grid * blocks + b + 1, :] = slot.astype(F32)
            group = slot >> 7
            place = slot & (LANES - 1)
            right[grid, :, lanes] = jnp.where(
                small_iota((LANES, LANES), 0) == small(place), one, nothing
            )
            chosen = iota((groups, LANES), 0) == group
            fields = [high[b : b + 1], low[b : b + 1]]
            fields += [piece[d : d + 1, lanes] for d in range(3) for piece in pieces]
            for index, field in enumerate(fields):
                left[grid, index * groups : (index + 1) * groups, lanes] = jnp.where(
                    chosen, field, 0.0
                ).astype(BF16)
        packed = lax.dot_general(left[grid], right[grid], NT, preferred_element_type=F32)
        part = [packed[i * groups : (i + 1) * groups] for i in range(8)]
        request[:, 4 * grid, :] = part[0] * 256.0 + part[1]
        for d in range(3):
            request[:, 4 * grid + 1 + d, :] = part[2 + 2 * d] + part[3 + 2 * d]
    for copy in loads[6:]:
        copy.wait()


def table_kernel(
    span_y, slots, cells, tile, far_block,
    tile_main, tile_rest, block_main, block_rest, inner_edge, outer_edge,
    block, description, sems,
):
    blocks = cells.shape[0]
    load = pltpu.make_async_copy(far_block, block, sems.at[0])
    load.start()
    description[:blocks, :] = slots[blocks:, :]
    description[blocks:, :] = cells[...].astype(F32)
    odd = parity()
    components, rows, depth = tile.shape
    layer = components * span_y
    sent = []
    for k, (edge, side) in enumerate(((inner_edge, 1 - odd), (outer_edge, odd))):
        sent.append(
            pltpu.make_async_copy(description, edge.at[pl.ds(layer, 2 * blocks)], sems.at[1 + k])
        )
        for c in range(components):
            sent.append(
                pltpu.make_async_copy(
                    tile.at[c, pl.ds(pl.multiple_of(side * (rows - span_y), 8), span_y)],
                    edge.at[pl.ds(c * span_y, span_y)],
                    sems.at[3 + k * components + c],
                )
            )
    for copy in sent:
        copy.start()
    for source, main, rest in ((tile, tile_main, tile_rest), (block, block_main, block_rest)):
        if source is block:
            load.wait()
        rows = source.shape[1]
        for c in range(components):
            for start in range(0, rows, LANES):
                turned = source[c, start : start + LANES, :].T
                coarse = turned.astype(BF16)
                fine = (turned - coarse.astype(F32)) * FINE
                where = slice(c * depth, (c + 1) * depth)
                main[where, start : start + LANES] = coarse
                rest[where, start : start + LANES] = fine.astype(F8)
    for copy in sent:
        copy.wait()


def mark_cells(cells, hits, marks, span, planes, b):
    one, nothing = jnp.ones((), BF16), jnp.zeros((), BF16)
    lanes = slice(b * LANES, (b + 1) * LANES)
    cell = cells.astype(jnp.int32)
    z = cell % LANES
    row = cell // LANES
    y = row % span
    x = row // span
    marks[:, lanes] = jnp.where(small_iota((LANES, LANES), 0) == small(z), one, nothing).astype(F8)
    along = small_iota((span, LANES), 0)
    for index, plane in enumerate(planes):
        hit = small(jnp.where(x == plane, y, -1))
        hits[index * span : (index + 1) * span, lanes] = jnp.where(
            along == hit, one, nothing
        ).astype(F8)


def taken_of(hits, marks):
    return lax.dot_general(hits[...], marks[...], NT, preferred_element_type=F32).astype(BF16)


def rows_of(span):
    return span[0] * span[1]


def donor_kernel(
    spans, width, shared, nb_cells, bg_cells, request,
    tile_main, tile_rest, block_main, block_rest,
    values, nb_hits, bg_hits, nb_taken, bg_taken,
    tile_weights, tile_fines, tile_rough, block_weights, block_fines, block_rough, marks,
):
    senders = request.shape[0]
    step = width // LANES
    nothing = jnp.zeros((), BF16)
    blocks = nb_cells.shape[0]
    sets = (
        (nb_cells, nb_hits, marks.at[0], spans[1][1], range(spans[1][0])),
        (bg_cells, bg_hits, marks.at[1], spans[0][1], range(spans[0][0])),
    )
    for b in range(blocks):
        for cells, hits, mark, span, planes in sets:
            mark_cells(cells[b : b + 1, :], hits, mark, span, planes, b)
    nb_taken[...] = taken_of(nb_hits, marks.at[0])
    bg_taken[...] = taken_of(bg_hits, marks.at[1])
    for first in range(0, senders, step):
        for grid, (main, rest, rough, weights, fines) in enumerate((
            (tile_main, tile_rest, tile_rough, tile_weights, tile_fines),
            (block_main, block_rest, block_rough, block_weights, block_fines),
        )):
            if first == 0:
                rough[:, :rows_of(spans[grid])] = main[...].astype(F8)
                rough[:, rows_of(spans[grid]) :] = rest[...]
            span_x, span_y, span_z = spans[grid]
            rows = span_x * span_y
            fields = [
                jnp.concatenate(
                    [request[first + s, 4 * grid + f, :][None] for s in range(step)], axis=1
                )
                for f in range(4)
            ]
            base = fields[0].astype(jnp.int32)
            place_z = base % span_z
            row = base // span_z
            place_y = row % span_y
            place_x = row // span_y
            frac_x, frac_y, frac_z = fields[1:]
            along = small_iota((span_y, width), 0)
            lower = along == small(place_y)
            upper = along == small(place_y + 1)
            for x in range(span_x):
                factor = jnp.where(
                    place_x == x, 1.0 - frac_x, jnp.where(place_x == x - 1, frac_x, 0.0)
                )
                coarse = []
                fine = []
                for weight in (factor * (1.0 - frac_y), factor * frac_y):
                    coarse.append(weight.astype(BF16))
                    fine.append(((weight - coarse[-1].astype(F32)) * FINE).astype(BF16))
                main_weight = jnp.where(lower, coarse[0], jnp.where(upper, coarse[1], nothing))
                rest_weight = jnp.where(lower, fine[0], jnp.where(upper, fine[1], nothing))
                here = slice(x * span_y, (x + 1) * span_y)
                weights[here, :] = main_weight
                fines[here, :] = rest_weight.astype(F8)
                fines[rows + x * span_y : rows + (x + 1) * span_y, :] = main_weight.astype(F8)
            mixed = lax.dot_general(main[...], weights[...], NN, preferred_element_type=F32)
            extra = lax.dot_general(rough[...], fines[...], NN, preferred_element_type=F32)
            mixed = mixed + (1.0 / FINE) * extra
            along = iota((span_z, width), 0)
            weight_z = jnp.where(
                along == place_z, 1.0 - frac_z, jnp.where(along == place_z + 1, frac_z, 0.0)
            )
            for c in range(4):
                total = jnp.sum(
                    mixed[c * span_z : (c + 1) * span_z] * weight_z, axis=0, keepdims=True
                )
                for s in range(step):
                    sender = first + s
                    line = total[0, s * LANES : (s + 1) * LANES]
                    values[sender, 4 * grid + c, :] = line
                    if grid and shared:
                        values[sender ^ 1, 8 + c, :] = line
                        if 0 < sender < senders - 1:
                            values[((sender + 1) ^ 1) - 1, 12 + c, :] = line
                        else:
                            values[sender, 12 + c, :] = jnp.zeros((LANES,), F32)


def receive(k, slots, cells, returned, spots, depth):
    groups = returned.shape[0]
    blocks = slots.shape[0]
    lhs = []
    for c in range(4):
        lhs += split(returned[:, 4 * k + c, :], 2)
    lhs = jnp.concatenate([lhs[2 * c + s] for s in range(2) for c in range(4)], axis=0)
    size = 4 * groups
    one, nothing = jnp.ones((), BF16), jnp.zeros((), BF16)
    for b in range(blocks):
        lanes = slice(b * LANES, (b + 1) * LANES)
        slot = slots[b : b + 1].astype(jnp.int32)
        z = cells[b : b + 1].astype(jnp.int32) % depth
        group = slot >> 7
        place = slot & (LANES - 1)
        along = small_iota((LANES, LANES), 0)
        onehot = jnp.where(along == small(place), one, nothing)
        found = lax.dot_general(lhs, onehot, NN, preferred_element_type=F32)
        found = found[:size] + found[size:]
        chosen = iota((groups, LANES), 0) == group
        mark = along == small(z)
        for c in range(4):
            value = SCALE * jnp.sum(
                jnp.where(chosen, found[c * groups : (c + 1) * groups], 0.0),
                axis=0,
                keepdims=True,
            )
            for s in range(3):
                piece = value.astype(F8).astype(F32)
                value = value - piece
                spots[4 * s + c, :, lanes] = jnp.where(
                    mark, piece.astype(BF16), nothing
                ).astype(F8)


def place_values(hits, taken, spots, old, fields, rows, sources, targets):
    for c in range(0, 4, 2):
        placed = None
        for s in (0, 4, 8):
            pair = spots[s + c : s + c + 2].reshape(2 * LANES, -1)
            part = lax.dot_general(hits[...], pair, NT, preferred_element_type=F32)
            placed = part if placed is None else placed + part
        for index, (source, target) in enumerate(zip(sources, targets)):
            here = slice(index * rows, (index + 1) * rows)
            mask = taken[here, :].astype(F32) > 0.5
            for d in range(2):
                merged = jnp.where(
                    mask, (1.0 / SCALE) * placed[here, d * LANES : (d + 1) * LANES],
                    old[c + d, source],
                )
                fields[c + d, target, 8 : 8 + rows, :] = merged
                fields[c + d, target, 0:8, :] = merged[rows - 8 :]
                fields[c + d, target, 8 + rows :, :] = merged[:8]


def advance(fields, kappa, result, size, offset):
    for x in range(kappa.shape[0]):
        advance_plane(fields, kappa, result, size, offset, x)


def advance_plane(fields, kappa, result, size, offset, x):
    span_y, depth = kappa.shape[1:]
    lane = iota((size, depth), 1)
    count = fields.shape[1]
    if True:
        for start in range(0, span_y, size):
            scale = time_step * kappa[x, start : start + size, :]
            middle = slice(8 + start, 8 + start + size)
            speeds = [(-0.5 * time_step) * fields[d, x + offset, middle, :] for d in range(3)]
            for c in range(4):
                here = fields[c, x + offset, middle, :]
                left = fields[c, x + offset, 7 + start : 7 + start + size, :]
                right = fields[c, x + offset, 9 + start : 9 + start + size, :]
                up = jnp.where(lane == depth - 1, 0.0, pltpu.roll(here, depth - 1, 1))
                down = jnp.where(lane == 0, 0.0, pltpu.roll(here, 1, 1))
                total = (left + right) + (up + down) - 6.0 * here
                if x + offset == 0:
                    ahead = fields[c, x + offset + 1, middle, :]
                    total, slope = total + ahead, ahead
                elif x + offset == count - 1:
                    behind = fields[c, x + offset - 1, middle, :]
                    total, slope = total + behind, -behind
                else:
                    behind = fields[c, x + offset - 1, middle, :]
                    ahead = fields[c, x + offset + 1, middle, :]
                    total, slope = total + (behind + ahead), ahead - behind
                result[c, x, start : start + size, :] = (
                    here
                    + scale * total
                    + speeds[0] * slope
                    + speeds[1] * (right - left)
                    + speeds[2] * (up - down)
                )


def finish_kernel(
    returned, slots, nb_cells, bg_cells, nb_hits, bg_hits, nb_taken, bg_taken,
    inner, outer, background, near_body, bg_kappa, nb_kappa,
    new_background, new_near_body,
    tile_result, block_result, tile_fields, block_fields, spots, halo_hits, halo_taken, marks,
    sems,
):
    blocks, depth = nb_cells.shape[0], bg_kappa.shape[2]
    span_x, span_y = bg_kappa.shape[:2]
    block_x, block_y = nb_kappa.shape[:2]
    components = background.shape[0]
    layer = components * span_y
    odd = parity()
    receive(0, slots[:blocks, :], nb_cells[...], returned, spots.at[0], depth)
    receive(1, slots[blocks:, :], bg_cells[...], returned, spots.at[1], depth)
    for k, halo in ((2, inner), (3, outer)):
        receive(
            k, halo[layer : layer + blocks, :], halo[layer + blocks :, :], returned,
            spots.at[k], depth,
        )
    for k, (halo, plane) in enumerate(
        ((inner, odd * (span_x - 1)), (outer, (1 - odd) * (span_x - 1)))
    ):
        for b in range(blocks):
            cells = halo[layer + blocks + b : layer + blocks + b + 1, :]
            mark_cells(cells, halo_hits.at[k], marks.at[k], span_y, [plane], b)
        halo_taken[k] = taken_of(halo_hits.at[k], marks.at[k])
    place_values(
        nb_hits, nb_taken, spots.at[0], near_body, block_fields, block_y,
        range(block_x), range(block_x),
    )
    place_values(
        bg_hits, bg_taken, spots.at[1], background, tile_fields, span_y,
        range(span_x), range(1, span_x + 1),
    )
    advance(block_fields, nb_kappa, block_result, 32, 0)
    sent = [pltpu.make_async_copy(block_result, new_near_body, sems.at[0])]
    sent[0].start()
    for k, halo, target in (
        (0, inner, (1 - odd) * (span_x + 1)), (1, outer, odd * (span_x + 1)),
    ):
        old = halo.at[:layer, :].reshape(components, 1, span_y, depth)
        place_values(
            halo_hits.at[k], halo_taken.at[k], spots.at[2 + k], old, tile_fields, span_y,
            [0], [target],
        )
    for x in range(span_x):
        advance_plane(tile_fields, bg_kappa, tile_result, 32, 1, x)
        sent.append(
            pltpu.make_async_copy(tile_result.at[:, x], new_background.at[:, x], sems.at[1 + x])
        )
        sent[-1].start()
    for copy in sent:
        copy.wait()


def call(kernel, outs, scratch, flops, *operands, in_specs=None, out_specs=None):
    moved = sum(a.size * a.dtype.itemsize for a in operands)
    moved += sum(math.prod(o.shape) * jnp.dtype(o.dtype).itemsize for o in outs)
    specs = {}
    if in_specs is not None:
        specs = dict(in_specs=in_specs, out_specs=out_specs)
    return pl.pallas_call(
        kernel,
        out_shape=outs,
        scratch_shapes=scratch,
        compiler_params=pltpu.CompilerParams(vmem_limit_bytes=20 * MIB),
        cost_estimate=pl.CostEstimate(flops=flops, bytes_accessed=moved, transcendentals=0),
        **specs,
    )(*operands)


def distant(array):
    return pltpu.with_memory_space_constraint(array, pltpu.HBM)


def body(
    background, near_body, bg_kappa, nb_kappa,
    nb_recv_cell, nb_donor_owner, nb_donor_base, nb_donor_frac,
    bg_recv_cell, bg_donor_owner, bg_donor_base, bg_donor_frac,
):
    peers = lax.axis_size("tile")
    components, span_x, span_y, depth = background.shape
    block_x, block_y = near_body.shape[1:3]
    receptors = nb_recv_cell.shape[0]
    capacity = 2 * receptors // peers
    blocks = receptors // LANES
    groups = peers * capacity // LANES
    layer = components * span_y
    shape = jax.ShapeDtypeStruct

    def to_peers(array):
        if capacity == LANES:
            return array
        rows = array.shape[1]
        array = array.reshape(groups, rows, LANES // capacity, capacity)
        return array.transpose(0, 2, 1, 3).reshape(peers, rows, capacity)

    def to_groups(array):
        if capacity == LANES:
            return array
        rows = array.shape[1]
        array = array.reshape(groups, LANES // capacity, rows, capacity)
        return array.transpose(0, 2, 1, 3).reshape(groups, rows, LANES)

    def lines(array):
        return array.reshape(blocks, LANES)

    far = pl.BlockSpec(memory_space=pltpu.HBM)
    near = pl.BlockSpec(memory_space=pltpu.VMEM)
    rows = span_x * span_y
    block_rows = block_x * block_y
    edge = (layer + 2 * blocks, LANES)
    request, slots, nb_cells, bg_cells, tile = call(
        functools.partial(pack_kernel, peers, capacity),
        [
            shape((groups, 8, LANES), F32),
            shape((2 * blocks, LANES), F32),
            shape((blocks, LANES), jnp.int32),
            shape((blocks, LANES), jnp.int32),
            shape((components, rows, depth), F32),
        ],
        [
            pltpu.VMEM((4, blocks, LANES), jnp.int32),
            pltpu.VMEM((2, 3, receptors), F32),
            pltpu.VMEM((2, 8 * groups, receptors), BF16),
            pltpu.VMEM((2, LANES, receptors), BF16),
            pltpu.SemaphoreType.DMA((9,)),
        ],
        100_000_000,
        *(
            distant(operand)
            for operand in (
                lines(nb_donor_owner), lines(nb_donor_base), nb_donor_frac,
                lines(bg_donor_owner), lines(bg_donor_base), bg_donor_frac,
                lines(nb_recv_cell), lines(bg_recv_cell),
                background.reshape(components, rows, depth),
            )
        ),
        in_specs=[far] * 9,
        out_specs=[near] * 5,
    )
    request = to_groups(lax.all_to_all(to_peers(request), "tile", 0, 0, tiled=True))
    *tables, inner_edge, outer_edge = call(
        functools.partial(table_kernel, span_y),
        [
            shape((components * depth, rows), BF16),
            shape((components * depth, rows), F8),
            shape((components * depth, block_rows), BF16),
            shape((components * depth, block_rows), F8),
            pltpu.HBM(edge, F32),
            pltpu.HBM(edge, F32),
        ],
        [
            pltpu.VMEM((components, block_rows, depth), F32),
            pltpu.VMEM((2 * blocks, LANES), F32),
            pltpu.SemaphoreType.DMA((3 + 2 * components,)),
        ],
        1_000_000,
        slots, bg_cells, tile, distant(near_body.reshape(components, block_rows, depth)),
        in_specs=[near] * 3 + [far],
        out_specs=[near] * 4 + [far] * 2,
    )
    inner_pairs = [(i, i ^ 1) for i in range(peers)]
    outer_pairs = [(i, ((i + 1) ^ 1) - 1) for i in range(1, peers - 1)]
    inner = lax.ppermute(inner_edge, "tile", inner_pairs)
    outer = lax.ppermute(outer_edge, "tile", outer_pairs)
    width = 2 * LANES
    spans = ((span_x, span_y, depth), (block_x, block_y, depth))
    shared = capacity == LANES
    values, *found = call(
        functools.partial(donor_kernel, spans, width, shared),
        [
            shape((groups, 16 if shared else 8, LANES), F32),
            shape((block_rows, receptors), F8),
            shape((rows, receptors), F8),
            shape((block_rows, LANES), BF16),
            shape((rows, LANES), BF16),
        ],
        [
            pltpu.VMEM((rows, width), BF16),
            pltpu.VMEM((2 * rows, width), F8),
            pltpu.VMEM((components * depth, 2 * rows), F8),
            pltpu.VMEM((block_rows, width), BF16),
            pltpu.VMEM((2 * block_rows, width), F8),
            pltpu.VMEM((components * depth, 2 * block_rows), F8),
            pltpu.VMEM((2, depth, receptors), F8),
        ],
        20_000_000_000,
        nb_cells, bg_cells, request, *tables,
    )
    if not shared:
        values = to_peers(values)
        spare = values[:, 4:]
        tail = spare.shape[1:]
        empty = jnp.zeros((1,) + tail, F32)
        from_inner = jnp.flip(spare.reshape((peers // 2, 2) + tail), 1).reshape((peers,) + tail)
        middle = jnp.flip(spare[1:-1].reshape((peers // 2 - 1, 2) + tail), 1)
        from_outer = jnp.concatenate([empty, middle.reshape((peers - 2,) + tail), empty], axis=0)
        values = jnp.concatenate([values, from_inner, from_outer], axis=1)
    returned = to_groups(lax.all_to_all(values, "tile", 0, 0, tiled=True))

    return tuple(
        call(
            finish_kernel,
            [shape(background.shape, F32), shape(near_body.shape, F32)],
            [
                pltpu.VMEM(background.shape, F32),
                pltpu.VMEM(near_body.shape, F32),
                pltpu.VMEM((components, span_x + 2, span_y + 16, depth), F32),
                pltpu.VMEM((components, block_x, block_y + 16, depth), F32),
                pltpu.VMEM((4, 12, depth, receptors), F8),
                pltpu.VMEM((2, span_y, receptors), F8),
                pltpu.VMEM((2, span_y, LANES), BF16),
                pltpu.VMEM((2, depth, receptors), F8),
                pltpu.SemaphoreType.DMA((1 + span_x,)),
            ],
            2_000_000_000,
            returned, slots, nb_cells, bg_cells, *found, inner, outer,
            background, near_body, bg_kappa, nb_kappa,
            in_specs=[near] * 14,
            out_specs=[far] * 2,
        )
    )


def solution(mesh):
    both = ("group", "tile")
    field = P("group", "tile", None, None)
    row = (P(both), P(both, None), P(both), P(None, both))
    return jax.shard_map(
        body,
        mesh=mesh,
        in_specs=(field, field, P(both, None, None), P(both, None, None)) + row + row,
        out_specs=(field, field),
        check_vma=False,
    )
```

```python
import functools
import math

import jax
import jax.numpy as jnp
from jax import lax
from jax.experimental import pallas as pl
from jax.experimental.pallas import tpu as pltpu
from jax.sharding import PartitionSpec as P

time_step = 0.05
LANES = 128
F32 = jnp.float32
BF16 = jnp.bfloat16
F8 = jnp.float8_e4m3fn
FINE = 512.0
SCALE = 64.0
NT = (((1,), (1,)), ((), ()))
NN = (((1,), (0,)), ((), ()))
MIB = 1024 * 1024


def iota(shape, dim):
    return lax.broadcasted_iota(jnp.int32, shape, dim)


def small_iota(shape, dim):
    return iota(shape, dim).astype(F32).astype(BF16)


def small(value):
    return value.astype(F32).astype(BF16)


def split(value, pieces):
    result = []
    for _ in range(pieces):
        piece = value.astype(BF16)
        result.append(piece)
        value = value - piece.astype(F32)
    return result


def parity():
    return lax.rem(lax.axis_index("tile"), 2)


def pack_kernel(
    peers, capacity, nb_owner, nb_base, nb_frac, bg_owner, bg_base, bg_frac,
    nb_cell, bg_cell, far_tile, request, slots, nb_cells, bg_cells, tile,
    integers, fractions, left, right, sems,
):
    blocks = integers.shape[1]
    groups = request.shape[0]
    loads = [
        pltpu.make_async_copy(source, target, sems.at[i])
        for i, (source, target) in enumerate((
            (nb_owner, integers.at[0]), (nb_base, integers.at[1]), (nb_frac, fractions.at[0]),
            (bg_owner, integers.at[2]), (bg_base, integers.at[3]), (bg_frac, fractions.at[1]),
            (bg_cell, bg_cells), (nb_cell, nb_cells), (far_tile, tile),
        ))
    ]
    for copy in loads:
        copy.start()
    before = iota((LANES, 2 * LANES), 0) < iota((LANES, 2 * LANES), 1)
    triangle = jnp.where(before, 1.0, 0.0).astype(BF16)
    for copy in loads[:6]:
        copy.wait()
    one, nothing = jnp.ones((), BF16), jnp.zeros((), BF16)
    for grid in range(2):
        owners = integers[2 * grid]
        hits = [
            jnp.where(iota((peers, LANES), 0) == owners[b : b + 1], 1.0, 0.0)
            for b in range(blocks)
        ]
        counts = lax.dot_general(
            jnp.concatenate(hits, axis=0).astype(BF16), triangle, NN, preferred_element_type=F32
        )
        carry = jnp.zeros((peers, LANES), F32)
        bases = integers[2 * grid + 1]
        high = (bases >> 8).astype(F32)
        low = (bases & 255).astype(F32)
        pieces = []
        rest = fractions[grid]
        for _ in range(2):
            piece = rest.astype(BF16).astype(F32)
            pieces.append(piece)
            rest = rest - piece
        for b in range(blocks):
            part = slice(b * peers, (b + 1) * peers)
            lanes = slice(b * LANES, (b + 1) * LANES)
            running = counts[part, :LANES] + carry
            carry = carry + counts[part, LANES:]
            rank = jnp.sum(hits[b] * running, axis=0, keepdims=True).astype(jnp.int32)
            slot = owners[b : b + 1] * capacity + rank
            slots[grid * blocks + b : grid * blocks + b + 1, :] = slot.astype(F32)
            group = slot >> 7
            place = slot & (LANES - 1)
            right[grid, :, lanes] = jnp.where(
                small_iota((LANES, LANES), 0) == small(place), one, nothing
            )
            chosen = iota((groups, LANES), 0) == group
            fields = [high[b : b + 1], low[b : b + 1]]
            fields += [piece[d : d + 1, lanes] for d in range(3) for piece in pieces]
            for index, field in enumerate(fields):
                left[grid, index * groups : (index + 1) * groups, lanes] = jnp.where(
                    chosen, field, 0.0
                ).astype(BF16)
        packed = lax.dot_general(left[grid], right[grid], NT, preferred_element_type=F32)
        part = [packed[i * groups : (i + 1) * groups] for i in range(8)]
        request[:, 4 * grid, :] = part[0] * 256.0 + part[1]
        for d in range(3):
            request[:, 4 * grid + 1 + d, :] = part[2 + 2 * d] + part[3 + 2 * d]
    for copy in loads[6:]:
        copy.wait()


def table_kernel(
    span_y, slots, cells, tile, far_block,
    tile_main, tile_rest, block_main, block_rest, inner_edge, outer_edge,
    block, description, sems,
):
    blocks = cells.shape[0]
    load = pltpu.make_async_copy(far_block, block, sems.at[0])
    load.start()
    description[:blocks, :] = slots[blocks:, :]
    description[blocks:, :] = cells[...].astype(F32)
    odd = parity()
    components, rows, depth = tile.shape
    layer = components * span_y
    sent = []
    for k, (edge, side) in enumerate(((inner_edge, 1 - odd), (outer_edge, odd))):
        sent.append(
            pltpu.make_async_copy(description, edge.at[pl.ds(layer, 2 * blocks)], sems.at[1 + k])
        )
        for c in range(components):
            sent.append(
                pltpu.make_async_copy(
                    tile.at[c, pl.ds(pl.multiple_of(side * (rows - span_y), 8), span_y)],
                    edge.at[pl.ds(c * span_y, span_y)],
                    sems.at[3 + k * components + c],
                )
            )
    for copy in sent:
        copy.start()
    for source, main, rest in ((tile, tile_main, tile_rest), (block, block_main, block_rest)):
        if source is block:
            load.wait()
        rows = source.shape[1]
        for c in range(components):
            for start in range(0, rows, LANES):
                turned = source[c, start : start + LANES, :].T
                coarse = turned.astype(BF16)
                fine = (turned - coarse.astype(F32)) * FINE
                where = slice(c * depth, (c + 1) * depth)
                main[where, start : start + LANES] = coarse
                rest[where, start : start + LANES] = fine.astype(F8)
    for copy in sent:
        copy.wait()


def mark_cells(cells, hits, marks, span, planes, b):
    one, nothing = jnp.ones((), BF16), jnp.zeros((), BF16)
    lanes = slice(b * LANES, (b + 1) * LANES)
    cell = cells.astype(jnp.int32)
    z = cell % LANES
    row = cell // LANES
    y = row % span
    x = row // span
    marks[:, lanes] = jnp.where(small_iota((LANES, LANES), 0) == small(z), one, nothing).astype(F8)
    along = small_iota((span, LANES), 0)
    for index, plane in enumerate(planes):
        hit = small(jnp.where(x == plane, y, -1))
        hits[index * span : (index + 1) * span, lanes] = jnp.where(
            along == hit, one, nothing
        ).astype(F8)


def taken_of(hits, marks):
    return lax.dot_general(hits[...], marks[...], NT, preferred_element_type=F32).astype(BF16)


def rows_of(span):
    return span[0] * span[1]


def donor_kernel(
    spans, width, shared, nb_cells, bg_cells, request,
    tile_main, tile_rest, block_main, block_rest,
    values, nb_hits, bg_hits, nb_taken, bg_taken,
    tile_weights, tile_fines, tile_rough, block_weights, block_fines, block_rough, marks,
):
    senders = request.shape[0]
    step = width // LANES
    nothing = jnp.zeros((), BF16)
    blocks = nb_cells.shape[0]
    sets = (
        (nb_cells, nb_hits, marks.at[0], spans[1][1], range(spans[1][0])),
        (bg_cells, bg_hits, marks.at[1], spans[0][1], range(spans[0][0])),
    )
    for b in range(blocks):
        for cells, hits, mark, span, planes in sets:
            mark_cells(cells[b : b + 1, :], hits, mark, span, planes, b)
    nb_taken[...] = taken_of(nb_hits, marks.at[0])
    bg_taken[...] = taken_of(bg_hits, marks.at[1])
    for first in range(0, senders, step):
        for grid, (main, rest, rough, weights, fines) in enumerate((
            (tile_main, tile_rest, tile_rough, tile_weights, tile_fines),
            (block_main, block_rest, block_rough, block_weights, block_fines),
        )):
            if first == 0:
                rough[:, :rows_of(spans[grid])] = main[...].astype(F8)
                rough[:, rows_of(spans[grid]) :] = rest[...]
            span_x, span_y, span_z = spans[grid]
            rows = span_x * span_y
            fields = [
                jnp.concatenate(
                    [request[first + s, 4 * grid + f, :][None] for s in range(step)], axis=1
                )
                for f in range(4)
            ]
            base = fields[0].astype(jnp.int32)
            place_z = base % span_z
            row = base // span_z
            place_y = row % span_y
            place_x = row // span_y
            frac_x, frac_y, frac_z = fields[1:]
            along = small_iota((span_y, width), 0)
            lower = along == small(place_y)
            upper = along == small(place_y + 1)
            for x in range(span_x):
                factor = jnp.where(
                    place_x == x, 1.0 - frac_x, jnp.where(place_x == x - 1, frac_x, 0.0)
                )
                coarse = []
                fine = []
                for weight in (factor * (1.0 - frac_y), factor * frac_y):
                    coarse.append(weight.astype(BF16))
                    fine.append(((weight - coarse[-1].astype(F32)) * FINE).astype(BF16))
                main_weight = jnp.where(lower, coarse[0], jnp.where(upper, coarse[1], nothing))
                rest_weight = jnp.where(lower, fine[0], jnp.where(upper, fine[1], nothing))
                here = slice(x * span_y, (x + 1) * span_y)
                weights[here, :] = main_weight
                fines[here, :] = rest_weight.astype(F8)
                fines[rows + x * span_y : rows + (x + 1) * span_y, :] = main_weight.astype(F8)
            mixed = lax.dot_general(main[...], weights[...], NN, preferred_element_type=F32)
            extra = lax.dot_general(rough[...], fines[...], NN, preferred_element_type=F32)
            mixed = mixed + (1.0 / FINE) * extra
            along = iota((span_z, width), 0)
            weight_z = jnp.where(
                along == place_z, 1.0 - frac_z, jnp.where(along == place_z + 1, frac_z, 0.0)
            )
            for c in range(4):
                total = jnp.sum(
                    mixed[c * span_z : (c + 1) * span_z] * weight_z, axis=0, keepdims=True
                )
                for s in range(step):
                    sender = first + s
                    line = total[0, s * LANES : (s + 1) * LANES]
                    values[sender, 4 * grid + c, :] = line
                    if grid and shared:
                        values[sender ^ 1, 8 + c, :] = line
                        if 0 < sender < senders - 1:
                            values[((sender + 1) ^ 1) - 1, 12 + c, :] = line
                        else:
                            values[sender, 12 + c, :] = jnp.zeros((LANES,), F32)


def receive(k, slots, cells, returned, spots, depth):
    groups = returned.shape[0]
    blocks = slots.shape[0]
    lhs = []
    for c in range(4):
        lhs += split(returned[:, 4 * k + c, :], 2)
    lhs = jnp.concatenate([lhs[2 * c + s] for s in range(2) for c in range(4)], axis=0)
    size = 4 * groups
    one, nothing = jnp.ones((), BF16), jnp.zeros((), BF16)
    for b in range(blocks):
        lanes = slice(b * LANES, (b + 1) * LANES)
        slot = slots[b : b + 1].astype(jnp.int32)
        z = cells[b : b + 1].astype(jnp.int32) % depth
        group = slot >> 7
        place = slot & (LANES - 1)
        along = small_iota((LANES, LANES), 0)
        onehot = jnp.where(along == small(place), one, nothing)
        found = lax.dot_general(lhs, onehot, NN, preferred_element_type=F32)
        found = found[:size] + found[size:]
        chosen = iota((groups, LANES), 0) == group
        mark = along == small(z)
        for c in range(4):
            value = SCALE * jnp.sum(
                jnp.where(chosen, found[c * groups : (c + 1) * groups], 0.0),
                axis=0,
                keepdims=True,
            )
            for s in range(3):
                piece = value.astype(F8).astype(F32)
                value = value - piece
                spots[4 * s + c, :, lanes] = jnp.where(
                    mark, piece.astype(BF16), nothing
                ).astype(F8)


def place_values(hits, taken, spots, old, fields, rows, sources, targets):
    for c in range(0, 4, 2):
        placed = None
        for s in (0, 4, 8):
            pair = spots[s + c : s + c + 2].reshape(2 * LANES, -1)
            part = lax.dot_general(hits[...], pair, NT, preferred_element_type=F32)
            placed = part if placed is None else placed + part
        for index, (source, target) in enumerate(zip(sources, targets)):
            here = slice(index * rows, (index + 1) * rows)
            mask = taken[here, :].astype(F32) > 0.5
            for d in range(2):
                merged = jnp.where(
                    mask, (1.0 / SCALE) * placed[here, d * LANES : (d + 1) * LANES],
                    old[c + d, source],
                )
                fields[c + d, target, 8 : 8 + rows, :] = merged
                fields[c + d, target, 0:8, :] = merged[rows - 8 :]
                fields[c + d, target, 8 + rows :, :] = merged[:8]


def advance(fields, kappa, result, size, offset):
    for x in range(kappa.shape[0]):
        advance_plane(fields, kappa, result, size, offset, x, 0, kappa.shape[1])


def advance_plane(fields, kappa, result, size, offset, x, begin, end):
    depth = kappa.shape[2]
    lane = iota((size, depth), 1)
    count = fields.shape[1]
    for start in range(begin, end, size):
        scale = time_step * kappa[x, start : start + size, :]
        middle = slice(8 + start, 8 + start + size)
        speeds = [(-0.5 * time_step) * fields[d, x + offset, middle, :] for d in range(3)]
        for c in range(4):
            here = fields[c, x + offset, middle, :]
            left = fields[c, x + offset, 7 + start : 7 + start + size, :]
            right = fields[c, x + offset, 9 + start : 9 + start + size, :]
            up = jnp.where(lane == depth - 1, 0.0, pltpu.roll(here, depth - 1, 1))
            down = jnp.where(lane == 0, 0.0, pltpu.roll(here, 1, 1))
            total = (left + right) + (up + down) - 6.0 * here
            if x + offset == 0:
                ahead = fields[c, x + offset + 1, middle, :]
                total, slope = total + ahead, ahead
            elif x + offset == count - 1:
                behind = fields[c, x + offset - 1, middle, :]
                total, slope = total + behind, -behind
            else:
                behind = fields[c, x + offset - 1, middle, :]
                ahead = fields[c, x + offset + 1, middle, :]
                total, slope = total + (behind + ahead), ahead - behind
            result[c, x, start : start + size, :] = (
                here
                + scale * total
                + speeds[0] * slope
                + speeds[1] * (right - left)
                + speeds[2] * (up - down)
            )


def finish_kernel(
    returned, slots, nb_cells, bg_cells, nb_hits, bg_hits, nb_taken, bg_taken,
    inner, outer, background, near_body, bg_kappa, nb_kappa,
    new_background, new_near_body,
    tile_result, block_result, tile_fields, block_fields, spots, halo_hits, halo_taken, marks,
    sems,
):
    blocks, depth = nb_cells.shape[0], bg_kappa.shape[2]
    span_x, span_y = bg_kappa.shape[:2]
    block_x, block_y = nb_kappa.shape[:2]
    components = background.shape[0]
    layer = components * span_y
    odd = parity()
    receive(0, slots[:blocks, :], nb_cells[...], returned, spots.at[0], depth)
    receive(1, slots[blocks:, :], bg_cells[...], returned, spots.at[1], depth)
    for k, halo in ((2, inner), (3, outer)):
        receive(
            k, halo[layer : layer + blocks, :], halo[layer + blocks :, :], returned,
            spots.at[k], depth,
        )
    for k, (halo, plane) in enumerate(
        ((inner, odd * (span_x - 1)), (outer, (1 - odd) * (span_x - 1)))
    ):
        for b in range(blocks):
            cells = halo[layer + blocks + b : layer + blocks + b + 1, :]
            mark_cells(cells, halo_hits.at[k], marks.at[k], span_y, [plane], b)
        halo_taken[k] = taken_of(halo_hits.at[k], marks.at[k])
    place_values(
        nb_hits, nb_taken, spots.at[0], near_body, block_fields, block_y,
        range(block_x), range(block_x),
    )
    place_values(
        bg_hits, bg_taken, spots.at[1], background, tile_fields, span_y,
        range(span_x), range(1, span_x + 1),
    )
    advance(block_fields, nb_kappa, block_result, 32, 0)
    sent = [pltpu.make_async_copy(block_result, new_near_body, sems.at[0])]
    sent[0].start()
    for k, halo, target in (
        (0, inner, (1 - odd) * (span_x + 1)), (1, outer, odd * (span_x + 1)),
    ):
        old = halo.at[:layer, :].reshape(components, 1, span_y, depth)
        place_values(
            halo_hits.at[k], halo_taken.at[k], spots.at[2 + k], old, tile_fields, span_y,
            [0], [target],
        )
    part = span_y // 4
    for x in range(span_x):
        for k in range(4):
            advance_plane(tile_fields, bg_kappa, tile_result, 32, 1, x, k * part, (k + 1) * part)
            here = pl.ds(k * part, part)
            sent.append(
                pltpu.make_async_copy(
                    tile_result.at[:, x, here], new_background.at[:, x, here],
                    sems.at[1 + 4 * x + k],
                )
            )
            sent[-1].start()
    for copy in sent:
        copy.wait()


def call(kernel, outs, scratch, flops, *operands, in_specs=None, out_specs=None):
    moved = sum(a.size * a.dtype.itemsize for a in operands)
    moved += sum(math.prod(o.shape) * jnp.dtype(o.dtype).itemsize for o in outs)
    specs = {}
    if in_specs is not None:
        specs = dict(in_specs=in_specs, out_specs=out_specs)
    return pl.pallas_call(
        kernel,
        out_shape=outs,
        scratch_shapes=scratch,
        compiler_params=pltpu.CompilerParams(vmem_limit_bytes=20 * MIB),
        cost_estimate=pl.CostEstimate(flops=flops, bytes_accessed=moved, transcendentals=0),
        **specs,
    )(*operands)


def distant(array):
    return pltpu.with_memory_space_constraint(array, pltpu.HBM)


def body(
    background, near_body, bg_kappa, nb_kappa,
    nb_recv_cell, nb_donor_owner, nb_donor_base, nb_donor_frac,
    bg_recv_cell, bg_donor_owner, bg_donor_base, bg_donor_frac,
):
    peers = lax.axis_size("tile")
    components, span_x, span_y, depth = background.shape
    block_x, block_y = near_body.shape[1:3]
    receptors = nb_recv_cell.shape[0]
    capacity = 2 * receptors // peers
    blocks = receptors // LANES
    groups = peers * capacity // LANES
    layer = components * span_y
    shape = jax.ShapeDtypeStruct

    def to_peers(array):
        if capacity == LANES:
            return array
        rows = array.shape[1]
        array = array.reshape(groups, rows, LANES // capacity, capacity)
        return array.transpose(0, 2, 1, 3).reshape(peers, rows, capacity)

    def to_groups(array):
        if capacity == LANES:
            return array
        rows = array.shape[1]
        array = array.reshape(groups, LANES // capacity, rows, capacity)
        return array.transpose(0, 2, 1, 3).reshape(groups, rows, LANES)

    def lines(array):
        return array.reshape(blocks, LANES)

    far = pl.BlockSpec(memory_space=pltpu.HBM)
    near = pl.BlockSpec(memory_space=pltpu.VMEM)
    rows = span_x * span_y
    block_rows = block_x * block_y
    edge = (layer + 2 * blocks, LANES)
    request, slots, nb_cells, bg_cells, tile = call(
        functools.partial(pack_kernel, peers, capacity),
        [
            shape((groups, 8, LANES), F32),
            shape((2 * blocks, LANES), F32),
            shape((blocks, LANES), jnp.int32),
            shape((blocks, LANES), jnp.int32),
            shape((components, rows, depth), F32),
        ],
        [
            pltpu.VMEM((4, blocks, LANES), jnp.int32),
            pltpu.VMEM((2, 3, receptors), F32),
            pltpu.VMEM((2, 8 * groups, receptors), BF16),
            pltpu.VMEM((2, LANES, receptors), BF16),
            pltpu.SemaphoreType.DMA((9,)),
        ],
        100_000_000,
        *(
            distant(operand)
            for operand in (
                lines(nb_donor_owner), lines(nb_donor_base), nb_donor_frac,
                lines(bg_donor_owner), lines(bg_donor_base), bg_donor_frac,
                lines(nb_recv_cell), lines(bg_recv_cell),
                background.reshape(components, rows, depth),
            )
        ),
        in_specs=[far] * 9,
        out_specs=[near] * 5,
    )
    request = to_groups(lax.all_to_all(to_peers(request), "tile", 0, 0, tiled=True))
    *tables, inner_edge, outer_edge = call(
        functools.partial(table_kernel, span_y),
        [
            shape((components * depth, rows), BF16),
            shape((components * depth, rows), F8),
            shape((components * depth, block_rows), BF16),
            shape((components * depth, block_rows), F8),
            pltpu.HBM(edge, F32),
            pltpu.HBM(edge, F32),
        ],
        [
            pltpu.VMEM((components, block_rows, depth), F32),
            pltpu.VMEM((2 * blocks, LANES), F32),
            pltpu.SemaphoreType.DMA((3 + 2 * components,)),
        ],
        1_000_000,
        slots, bg_cells, tile, distant(near_body.reshape(components, block_rows, depth)),
        in_specs=[near] * 3 + [far],
        out_specs=[near] * 4 + [far] * 2,
    )
    inner_pairs = [(i, i ^ 1) for i in range(peers)]
    outer_pairs = [(i, ((i + 1) ^ 1) - 1) for i in range(1, peers - 1)]
    inner = lax.ppermute(inner_edge, "tile", inner_pairs)
    outer = lax.ppermute(outer_edge, "tile", outer_pairs)
    width = 2 * LANES
    spans = ((span_x, span_y, depth), (block_x, block_y, depth))
    shared = capacity == LANES
    values, *found = call(
        functools.partial(donor_kernel, spans, width, shared),
        [
            shape((groups, 16 if shared else 8, LANES), F32),
            shape((block_rows, receptors), F8),
            shape((rows, receptors), F8),
            shape((block_rows, LANES), BF16),
            shape((rows, LANES), BF16),
        ],
        [
            pltpu.VMEM((rows, width), BF16),
            pltpu.VMEM((2 * rows, width), F8),
            pltpu.VMEM((components * depth, 2 * rows), F8),
            pltpu.VMEM((block_rows, width), BF16),
            pltpu.VMEM((2 * block_rows, width), F8),
            pltpu.VMEM((components * depth, 2 * block_rows), F8),
            pltpu.VMEM((2, depth, receptors), F8),
        ],
        20_000_000_000,
        nb_cells, bg_cells, request, *tables,
    )
    if not shared:
        values = to_peers(values)
        spare = values[:, 4:]
        tail = spare.shape[1:]
        empty = jnp.zeros((1,) + tail, F32)
        from_inner = jnp.flip(spare.reshape((peers // 2, 2) + tail), 1).reshape((peers,) + tail)
        middle = jnp.flip(spare[1:-1].reshape((peers // 2 - 1, 2) + tail), 1)
        from_outer = jnp.concatenate([empty, middle.reshape((peers - 2,) + tail), empty], axis=0)
        values = jnp.concatenate([values, from_inner, from_outer], axis=1)
    returned = to_groups(lax.all_to_all(values, "tile", 0, 0, tiled=True))

    return tuple(
        call(
            finish_kernel,
            [shape(background.shape, F32), shape(near_body.shape, F32)],
            [
                pltpu.VMEM(background.shape, F32),
                pltpu.VMEM(near_body.shape, F32),
                pltpu.VMEM((components, span_x + 2, span_y + 16, depth), F32),
                pltpu.VMEM((components, block_x, block_y + 16, depth), F32),
                pltpu.VMEM((4, 12, depth, receptors), F8),
                pltpu.VMEM((2, span_y, receptors), F8),
                pltpu.VMEM((2, span_y, LANES), BF16),
                pltpu.VMEM((2, depth, receptors), F8),
                pltpu.SemaphoreType.DMA((1 + 4 * span_x,)),
            ],
            2_000_000_000,
            returned, slots, nb_cells, bg_cells, *found, inner, outer,
            background, near_body, bg_kappa, nb_kappa,
            in_specs=[near] * 14,
            out_specs=[far] * 2,
        )
    )


def solution(mesh):
    both = ("group", "tile")
    field = P("group", "tile", None, None)
    row = (P(both), P(both, None), P(both), P(None, both))
    return jax.shard_map(
        body,
        mesh=mesh,
        in_specs=(field, field, P(both, None, None), P(both, None, None)) + row + row,
        out_specs=(field, field),
        check_vma=False,
    )
```

```python
import functools
import math

import jax
import jax.numpy as jnp
from jax import lax
from jax.experimental import pallas as pl
from jax.experimental.pallas import tpu as pltpu
from jax.sharding import PartitionSpec as P

time_step = 0.05
LANES = 128
F32 = jnp.float32
BF16 = jnp.bfloat16
F8 = jnp.float8_e4m3fn
FINE = 512.0
SCALE = 64.0
NT = (((1,), (1,)), ((), ()))
NN = (((1,), (0,)), ((), ()))
MIB = 1024 * 1024


def iota(shape, dim):
    return lax.broadcasted_iota(jnp.int32, shape, dim)


def small_iota(shape, dim):
    return iota(shape, dim).astype(F32).astype(BF16)


def small(value):
    return value.astype(F32).astype(BF16)


def split(value, pieces):
    result = []
    for _ in range(pieces):
        piece = value.astype(BF16)
        result.append(piece)
        value = value - piece.astype(F32)
    return result


def parity():
    return lax.rem(lax.axis_index("tile"), 2)


def pack_kernel(
    peers, capacity, nb_owner, nb_base, nb_frac, bg_owner, bg_base, bg_frac,
    nb_cell, bg_cell, far_tile, request, slots, nb_cells, bg_cells, tile,
    integers, fractions, left, right, sems,
):
    blocks = integers.shape[1]
    groups = request.shape[0]
    loads = [
        pltpu.make_async_copy(source, target, sems.at[i])
        for i, (source, target) in enumerate((
            (nb_owner, integers.at[0]), (nb_base, integers.at[1]), (nb_frac, fractions.at[0]),
            (bg_owner, integers.at[2]), (bg_base, integers.at[3]), (bg_frac, fractions.at[1]),
            (bg_cell, bg_cells), (nb_cell, nb_cells), (far_tile, tile),
        ))
    ]
    for copy in loads:
        copy.start()
    before = iota((LANES, 2 * LANES), 0) < iota((LANES, 2 * LANES), 1)
    triangle = jnp.where(before, 1.0, 0.0).astype(BF16)
    for copy in loads[:6]:
        copy.wait()
    one, nothing = jnp.ones((), BF16), jnp.zeros((), BF16)
    for grid in range(2):
        owners = integers[2 * grid]
        hits = [
            jnp.where(iota((peers, LANES), 0) == owners[b : b + 1], 1.0, 0.0)
            for b in range(blocks)
        ]
        counts = lax.dot_general(
            jnp.concatenate(hits, axis=0).astype(BF16), triangle, NN, preferred_element_type=F32
        )
        carry = jnp.zeros((peers, LANES), F32)
        bases = integers[2 * grid + 1]
        high = (bases >> 8).astype(F32)
        low = (bases & 255).astype(F32)
        pieces = []
        rest = fractions[grid]
        for _ in range(2):
            piece = rest.astype(BF16).astype(F32)
            pieces.append(piece)
            rest = rest - piece
        for b in range(blocks):
            part = slice(b * peers, (b + 1) * peers)
            lanes = slice(b * LANES, (b + 1) * LANES)
            running = counts[part, :LANES] + carry
            carry = carry + counts[part, LANES:]
            rank = jnp.sum(hits[b] * running, axis=0, keepdims=True).astype(jnp.int32)
            slot = owners[b : b + 1] * capacity + rank
            slots[grid * blocks + b : grid * blocks + b + 1, :] = slot.astype(F32)
            group = slot >> 7
            place = slot & (LANES - 1)
            right[grid, :, lanes] = jnp.where(
                small_iota((LANES, LANES), 0) == small(place), one, nothing
            )
            chosen = iota((groups, LANES), 0) == group
            fields = [high[b : b + 1], low[b : b + 1]]
            fields += [piece[d : d + 1, lanes] for d in range(3) for piece in pieces]
            for index, field in enumerate(fields):
                left[grid, index * groups : (index + 1) * groups, lanes] = jnp.where(
                    chosen, field, 0.0
                ).astype(BF16)
        packed = lax.dot_general(left[grid], right[grid], NT, preferred_element_type=F32)
        part = [packed[i * groups : (i + 1) * groups] for i in range(8)]
        request[:, 4 * grid, :] = part[0] * 256.0 + part[1]
        for d in range(3):
            request[:, 4 * grid + 1 + d, :] = part[2 + 2 * d] + part[3 + 2 * d]
    for copy in loads[6:]:
        copy.wait()


def table_kernel(
    span_y, slots, cells, tile, far_block,
    tile_main, tile_rest, block_main, block_rest, inner_edge, outer_edge,
    block, description, sems,
):
    blocks = cells.shape[0]
    load = pltpu.make_async_copy(far_block, block, sems.at[0])
    load.start()
    description[:blocks, :] = slots[blocks:, :]
    description[blocks:, :] = cells[...].astype(F32)
    odd = parity()
    components, rows, depth = tile.shape
    layer = components * span_y
    sent = []
    for k, (edge, side) in enumerate(((inner_edge, 1 - odd), (outer_edge, odd))):
        sent.append(
            pltpu.make_async_copy(description, edge.at[pl.ds(layer, 2 * blocks)], sems.at[1 + k])
        )
        for c in range(components):
            sent.append(
                pltpu.make_async_copy(
                    tile.at[c, pl.ds(pl.multiple_of(side * (rows - span_y), 8), span_y)],
                    edge.at[pl.ds(c * span_y, span_y)],
                    sems.at[3 + k * components + c],
                )
            )
    for copy in sent:
        copy.start()
    for source, main, rest in ((tile, tile_main, tile_rest), (block, block_main, block_rest)):
        if source is block:
            load.wait()
        rows = source.shape[1]
        for c in range(components):
            for start in range(0, rows, LANES):
                turned = source[c, start : start + LANES, :].T
                coarse = turned.astype(BF16)
                fine = (turned - coarse.astype(F32)) * FINE
                where = slice(c * depth, (c + 1) * depth)
                main[where, start : start + LANES] = coarse
                rest[where, start : start + LANES] = fine.astype(F8)
    for copy in sent:
        copy.wait()


def mark_cells(cells, hits, marks, span, planes, b):
    one, nothing = jnp.ones((), BF16), jnp.zeros((), BF16)
    lanes = slice(b * LANES, (b + 1) * LANES)
    cell = cells.astype(jnp.int32)
    z = cell % LANES
    row = cell // LANES
    y = row % span
    x = row // span
    marks[:, lanes] = jnp.where(small_iota((LANES, LANES), 0) == small(z), one, nothing).astype(F8)
    along = small_iota((span, LANES), 0)
    for index, plane in enumerate(planes):
        hit = small(jnp.where(x == plane, y, -1))
        hits[index * span : (index + 1) * span, lanes] = jnp.where(
            along == hit, one, nothing
        ).astype(F8)


def taken_of(hits, marks):
    return lax.dot_general(hits[...], marks[...], NT, preferred_element_type=F32).astype(BF16)


def rows_of(span):
    return span[0] * span[1]


def donor_kernel(
    spans, width, shared, nb_cells, bg_cells, request,
    tile_main, tile_rest, block_main, block_rest,
    values, nb_hits, bg_hits, nb_taken, bg_taken,
    tile_weights, tile_fines, tile_rough, block_weights, block_fines, block_rough, marks,
):
    senders = request.shape[0]
    step = width // LANES
    nothing = jnp.zeros((), BF16)
    blocks = nb_cells.shape[0]
    sets = (
        (nb_cells, nb_hits, marks.at[0], spans[1][1], range(spans[1][0])),
        (bg_cells, bg_hits, marks.at[1], spans[0][1], range(spans[0][0])),
    )
    for b in range(blocks):
        for cells, hits, mark, span, planes in sets:
            mark_cells(cells[b : b + 1, :], hits, mark, span, planes, b)
    nb_taken[...] = taken_of(nb_hits, marks.at[0])
    bg_taken[...] = taken_of(bg_hits, marks.at[1])
    for first in range(0, senders, step):
        for grid, (main, rest, rough, weights, fines) in enumerate((
            (tile_main, tile_rest, tile_rough, tile_weights, tile_fines),
            (block_main, block_rest, block_rough, block_weights, block_fines),
        )):
            if first == 0:
                rough[:, :rows_of(spans[grid])] = main[...].astype(F8)
                rough[:, rows_of(spans[grid]) :] = rest[...]
            span_x, span_y, span_z = spans[grid]
            rows = span_x * span_y
            fields = [
                jnp.concatenate(
                    [request[first + s, 4 * grid + f, :][None] for s in range(step)], axis=1
                )
                for f in range(4)
            ]
            base = fields[0].astype(jnp.int32)
            place_z = base % span_z
            row = base // span_z
            place_y = row % span_y
            place_x = row // span_y
            frac_x, frac_y, frac_z = fields[1:]
            along = small_iota((span_y, width), 0)
            lower = along == small(place_y)
            upper = along == small(place_y + 1)
            for x in range(span_x):
                factor = jnp.where(
                    place_x == x, 1.0 - frac_x, jnp.where(place_x == x - 1, frac_x, 0.0)
                )
                coarse = []
                fine = []
                for weight in (factor * (1.0 - frac_y), factor * frac_y):
                    coarse.append(weight.astype(BF16))
                    fine.append(((weight - coarse[-1].astype(F32)) * FINE).astype(BF16))
                main_weight = jnp.where(lower, coarse[0], jnp.where(upper, coarse[1], nothing))
                rest_weight = jnp.where(lower, fine[0], jnp.where(upper, fine[1], nothing))
                here = slice(x * span_y, (x + 1) * span_y)
                weights[here, :] = main_weight
                fines[here, :] = rest_weight.astype(F8)
                fines[rows + x * span_y : rows + (x + 1) * span_y, :] = main_weight.astype(F8)
            mixed = lax.dot_general(main[...], weights[...], NN, preferred_element_type=F32)
            extra = lax.dot_general(rough[...], fines[...], NN, preferred_element_type=F32)
            mixed = mixed + (1.0 / FINE) * extra
            along = iota((span_z, width), 0)
            weight_z = jnp.where(
                along == place_z, 1.0 - frac_z, jnp.where(along == place_z + 1, frac_z, 0.0)
            )
            for c in range(4):
                total = jnp.sum(
                    mixed[c * span_z : (c + 1) * span_z] * weight_z, axis=0, keepdims=True
                )
                for s in range(step):
                    sender = first + s
                    line = total[0, s * LANES : (s + 1) * LANES]
                    values[sender, 4 * grid + c, :] = line
                    if grid and shared:
                        values[sender ^ 1, 8 + c, :] = line
                        if 0 < sender < senders - 1:
                            values[((sender + 1) ^ 1) - 1, 12 + c, :] = line
                        else:
                            values[sender, 12 + c, :] = jnp.zeros((LANES,), F32)


def receive(k, slots, cells, returned, spots, depth):
    groups = returned.shape[0]
    blocks = slots.shape[0]
    lhs = []
    for c in range(4):
        lhs += split(returned[:, 4 * k + c, :], 2)
    lhs = jnp.concatenate([lhs[2 * c + s] for s in range(2) for c in range(4)], axis=0)
    size = 4 * groups
    one, nothing = jnp.ones((), BF16), jnp.zeros((), BF16)
    for b in range(blocks):
        lanes = slice(b * LANES, (b + 1) * LANES)
        slot = slots[b : b + 1].astype(jnp.int32)
        z = cells[b : b + 1].astype(jnp.int32) % depth
        group = slot >> 7
        place = slot & (LANES - 1)
        along = small_iota((LANES, LANES), 0)
        onehot = jnp.where(along == small(place), one, nothing)
        found = lax.dot_general(lhs, onehot, NN, preferred_element_type=F32)
        found = found[:size] + found[size:]
        chosen = iota((groups, LANES), 0) == group
        mark = along == small(z)
        for c in range(4):
            value = SCALE * jnp.sum(
                jnp.where(chosen, found[c * groups : (c + 1) * groups], 0.0),
                axis=0,
                keepdims=True,
            )
            for s in range(3):
                piece = value.astype(F8).astype(F32)
                value = value - piece
                spots[4 * s + c, :, lanes] = jnp.where(
                    mark, piece.astype(BF16), nothing
                ).astype(F8)


def place_values(hits, taken, spots, old, fields, rows, sources, targets):
    for c in range(0, 4, 2):
        placed = None
        for s in (0, 4, 8):
            pair = spots[s + c : s + c + 2].reshape(2 * LANES, -1)
            part = lax.dot_general(hits[...], pair, NT, preferred_element_type=F32)
            placed = part if placed is None else placed + part
        for index, (source, target) in enumerate(zip(sources, targets)):
            here = slice(index * rows, (index + 1) * rows)
            mask = taken[here, :].astype(F32) > 0.5
            for d in range(2):
                merged = jnp.where(
                    mask, (1.0 / SCALE) * placed[here, d * LANES : (d + 1) * LANES],
                    old[c + d, source],
                )
                fields[c + d, target, 8 : 8 + rows, :] = merged
                fields[c + d, target, 0:8, :] = merged[rows - 8 :]
                fields[c + d, target, 8 + rows :, :] = merged[:8]


def advance(fields, kappa, result, size, offset):
    for x in range(kappa.shape[0]):
        advance_plane(fields, kappa, result, size, offset, x, 0, kappa.shape[1])


def advance_plane(fields, kappa, result, size, offset, x, begin, end):
    depth = kappa.shape[2]
    lane = iota((size, depth), 1)
    count = fields.shape[1]
    for start in range(begin, end, size):
        scale = time_step * kappa[x, start : start + size, :]
        middle = slice(8 + start, 8 + start + size)
        speeds = [(0.5 * time_step) * fields[d, x + offset, middle, :] for d in range(3)]
        centre = 1.0 - 6.0 * scale
        to_ahead, to_behind = scale - speeds[0], scale + speeds[0]
        to_right, to_left = scale - speeds[1], scale + speeds[1]
        to_up = jnp.where(lane == depth - 1, 0.0, scale - speeds[2])
        to_down = jnp.where(lane == 0, 0.0, scale + speeds[2])
        for c in range(4):
            here = fields[c, x + offset, middle, :]
            left = fields[c, x + offset, 7 + start : 7 + start + size, :]
            right = fields[c, x + offset, 9 + start : 9 + start + size, :]
            total = (centre * here + to_right * right) + to_left * left
            total = total + (
                to_up * pltpu.roll(here, depth - 1, 1) + to_down * pltpu.roll(here, 1, 1)
            )
            if x + offset > 0:
                total = total + to_behind * fields[c, x + offset - 1, middle, :]
            if x + offset < count - 1:
                total = total + to_ahead * fields[c, x + offset + 1, middle, :]
            result[c, x, start : start + size, :] = total


def finish_kernel(
    returned, slots, nb_cells, bg_cells, nb_hits, bg_hits, nb_taken, bg_taken,
    inner, outer, background, near_body, bg_kappa, nb_kappa,
    new_background, new_near_body,
    tile_result, block_result, tile_fields, block_fields, spots, halo_hits, halo_taken, marks,
    sems,
):
    blocks, depth = nb_cells.shape[0], bg_kappa.shape[2]
    span_x, span_y = bg_kappa.shape[:2]
    block_x, block_y = nb_kappa.shape[:2]
    components = background.shape[0]
    layer = components * span_y
    odd = parity()
    receive(0, slots[:blocks, :], nb_cells[...], returned, spots.at[0], depth)
    receive(1, slots[blocks:, :], bg_cells[...], returned, spots.at[1], depth)
    for k, halo in ((2, inner), (3, outer)):
        receive(
            k, halo[layer : layer + blocks, :], halo[layer + blocks :, :], returned,
            spots.at[k], depth,
        )
    for k, (halo, plane) in enumerate(
        ((inner, odd * (span_x - 1)), (outer, (1 - odd) * (span_x - 1)))
    ):
        for b in range(blocks):
            cells = halo[layer + blocks + b : layer + blocks + b + 1, :]
            mark_cells(cells, halo_hits.at[k], marks.at[k], span_y, [plane], b)
        halo_taken[k] = taken_of(halo_hits.at[k], marks.at[k])
    place_values(
        nb_hits, nb_taken, spots.at[0], near_body, block_fields, block_y,
        range(block_x), range(block_x),
    )
    place_values(
        bg_hits, bg_taken, spots.at[1], background, tile_fields, span_y,
        range(span_x), range(1, span_x + 1),
    )
    advance(block_fields, nb_kappa, block_result, 8, 0)
    sent = [pltpu.make_async_copy(block_result, new_near_body, sems.at[0])]
    sent[0].start()
    for k, halo, target in (
        (0, inner, (1 - odd) * (span_x + 1)), (1, outer, odd * (span_x + 1)),
    ):
        old = halo.at[:layer, :].reshape(components, 1, span_y, depth)
        place_values(
            halo_hits.at[k], halo_taken.at[k], spots.at[2 + k], old, tile_fields, span_y,
            [0], [target],
        )
    part = span_y // 4
    for x in range(span_x):
        for k in range(4):
            advance_plane(tile_fields, bg_kappa, tile_result, 8, 1, x, k * part, (k + 1) * part)
            here = pl.ds(k * part, part)
            sent.append(
                pltpu.make_async_copy(
                    tile_result.at[:, x, here], new_background.at[:, x, here],
                    sems.at[1 + 4 * x + k],
                )
            )
            sent[-1].start()
    for copy in sent:
        copy.wait()


def call(kernel, outs, scratch, flops, *operands, in_specs=None, out_specs=None):
    moved = sum(a.size * a.dtype.itemsize for a in operands)
    moved += sum(math.prod(o.shape) * jnp.dtype(o.dtype).itemsize for o in outs)
    specs = {}
    if in_specs is not None:
        specs = dict(in_specs=in_specs, out_specs=out_specs)
    return pl.pallas_call(
        kernel,
        out_shape=outs,
        scratch_shapes=scratch,
        compiler_params=pltpu.CompilerParams(vmem_limit_bytes=20 * MIB),
        cost_estimate=pl.CostEstimate(flops=flops, bytes_accessed=moved, transcendentals=0),
        **specs,
    )(*operands)


def distant(array):
    return pltpu.with_memory_space_constraint(array, pltpu.HBM)


def body(
    background, near_body, bg_kappa, nb_kappa,
    nb_recv_cell, nb_donor_owner, nb_donor_base, nb_donor_frac,
    bg_recv_cell, bg_donor_owner, bg_donor_base, bg_donor_frac,
):
    peers = lax.axis_size("tile")
    components, span_x, span_y, depth = background.shape
    block_x, block_y = near_body.shape[1:3]
    receptors = nb_recv_cell.shape[0]
    capacity = 2 * receptors // peers
    blocks = receptors // LANES
    groups = peers * capacity // LANES
    layer = components * span_y
    shape = jax.ShapeDtypeStruct

    def to_peers(array):
        if capacity == LANES:
            return array
        rows = array.shape[1]
        array = array.reshape(groups, rows, LANES // capacity, capacity)
        return array.transpose(0, 2, 1, 3).reshape(peers, rows, capacity)

    def to_groups(array):
        if capacity == LANES:
            return array
        rows = array.shape[1]
        array = array.reshape(groups, LANES // capacity, rows, capacity)
        return array.transpose(0, 2, 1, 3).reshape(groups, rows, LANES)

    def lines(array):
        return array.reshape(blocks, LANES)

    far = pl.BlockSpec(memory_space=pltpu.HBM)
    near = pl.BlockSpec(memory_space=pltpu.VMEM)
    rows = span_x * span_y
    block_rows = block_x * block_y
    edge = (layer + 2 * blocks, LANES)
    request, slots, nb_cells, bg_cells, tile = call(
        functools.partial(pack_kernel, peers, capacity),
        [
            shape((groups, 8, LANES), F32),
            shape((2 * blocks, LANES), F32),
            shape((blocks, LANES), jnp.int32),
            shape((blocks, LANES), jnp.int32),
            shape((components, rows, depth), F32),
        ],
        [
            pltpu.VMEM((4, blocks, LANES), jnp.int32),
            pltpu.VMEM((2, 3, receptors), F32),
            pltpu.VMEM((2, 8 * groups, receptors), BF16),
            pltpu.VMEM((2, LANES, receptors), BF16),
            pltpu.SemaphoreType.DMA((9,)),
        ],
        100_000_000,
        *(
            distant(operand)
            for operand in (
                lines(nb_donor_owner), lines(nb_donor_base), nb_donor_frac,
                lines(bg_donor_owner), lines(bg_donor_base), bg_donor_frac,
                lines(nb_recv_cell), lines(bg_recv_cell),
                background.reshape(components, rows, depth),
            )
        ),
        in_specs=[far] * 9,
        out_specs=[near] * 5,
    )
    request = to_groups(lax.all_to_all(to_peers(request), "tile", 0, 0, tiled=True))
    *tables, inner_edge, outer_edge = call(
        functools.partial(table_kernel, span_y),
        [
            shape((components * depth, rows), BF16),
            shape((components * depth, rows), F8),
            shape((components * depth, block_rows), BF16),
            shape((components * depth, block_rows), F8),
            pltpu.HBM(edge, F32),
            pltpu.HBM(edge, F32),
        ],
        [
            pltpu.VMEM((components, block_rows, depth), F32),
            pltpu.VMEM((2 * blocks, LANES), F32),
            pltpu.SemaphoreType.DMA((3 + 2 * components,)),
        ],
        1_000_000,
        slots, bg_cells, tile, distant(near_body.reshape(components, block_rows, depth)),
        in_specs=[near] * 3 + [far],
        out_specs=[near] * 4 + [far] * 2,
    )
    inner_pairs = [(i, i ^ 1) for i in range(peers)]
    outer_pairs = [(i, ((i + 1) ^ 1) - 1) for i in range(1, peers - 1)]
    inner = lax.ppermute(inner_edge, "tile", inner_pairs)
    outer = lax.ppermute(outer_edge, "tile", outer_pairs)
    width = 2 * LANES
    spans = ((span_x, span_y, depth), (block_x, block_y, depth))
    shared = capacity == LANES
    values, *found = call(
        functools.partial(donor_kernel, spans, width, shared),
        [
            shape((groups, 16 if shared else 8, LANES), F32),
            shape((block_rows, receptors), F8),
            shape((rows, receptors), F8),
            shape((block_rows, LANES), BF16),
            shape((rows, LANES), BF16),
        ],
        [
            pltpu.VMEM((rows, width), BF16),
            pltpu.VMEM((2 * rows, width), F8),
            pltpu.VMEM((components * depth, 2 * rows), F8),
            pltpu.VMEM((block_rows, width), BF16),
            pltpu.VMEM((2 * block_rows, width), F8),
            pltpu.VMEM((components * depth, 2 * block_rows), F8),
            pltpu.VMEM((2, depth, receptors), F8),
        ],
        20_000_000_000,
        nb_cells, bg_cells, request, *tables,
    )
    if not shared:
        values = to_peers(values)
        spare = values[:, 4:]
        tail = spare.shape[1:]
        empty = jnp.zeros((1,) + tail, F32)
        from_inner = jnp.flip(spare.reshape((peers // 2, 2) + tail), 1).reshape((peers,) + tail)
        middle = jnp.flip(spare[1:-1].reshape((peers // 2 - 1, 2) + tail), 1)
        from_outer = jnp.concatenate([empty, middle.reshape((peers - 2,) + tail), empty], axis=0)
        values = jnp.concatenate([values, from_inner, from_outer], axis=1)
    returned = to_groups(lax.all_to_all(values, "tile", 0, 0, tiled=True))

    return tuple(
        call(
            finish_kernel,
            [shape(background.shape, F32), shape(near_body.shape, F32)],
            [
                pltpu.VMEM(background.shape, F32),
                pltpu.VMEM(near_body.shape, F32),
                pltpu.VMEM((components, span_x + 2, span_y + 16, depth), F32),
                pltpu.VMEM((components, block_x, block_y + 16, depth), F32),
                pltpu.VMEM((4, 12, depth, receptors), F8),
                pltpu.VMEM((2, span_y, receptors), F8),
                pltpu.VMEM((2, span_y, LANES), BF16),
                pltpu.VMEM((2, depth, receptors), F8),
                pltpu.SemaphoreType.DMA((1 + 4 * span_x,)),
            ],
            2_000_000_000,
            returned, slots, nb_cells, bg_cells, *found, inner, outer,
            background, near_body, bg_kappa, nb_kappa,
            in_specs=[near] * 14,
            out_specs=[far] * 2,
        )
    )


def solution(mesh):
    both = ("group", "tile")
    field = P("group", "tile", None, None)
    row = (P(both), P(both, None), P(both), P(None, both))
    return jax.shard_map(
        body,
        mesh=mesh,
        in_specs=(field, field, P(both, None, None), P(both, None, None)) + row + row,
        out_specs=(field, field),
        check_vma=False,
    )
```
